512 devices in a mesh: group: 16 (over y, x_lo, core), dev: 32 (over x_hi, z).
Axes of the slice: x: 4 (x_hi: 2, x_lo: 2; x = x_hi * 2 + x_lo), y: 4, z: 16, core: 2. Of those that a mesh axis runs over, the one named last changes fastest.
Arguments:
- prefill_pool: bfloat16 [512, 256, 2048], P('group', 'dev'), may hold values from -6 to 6
- page_table: int32 [16, 32, 32], P('group', 'dev'), may hold values from 0 to 31, each once within a row
- req_lengths: int32 [128], P('group'), may hold values from 1 to 1024, as said below
- dest_group: int32 [128], P('group'), may hold values from 0 to 15, as said below
- resident_kv: bfloat16 [64, 16384, 256], P('group', 'dev'), may hold values from -6 to 6
- resident_scale: bfloat16 [64, 16384, 2], P('group', 'dev'), may hold values from 0.25 to 4
- res_lengths: int32 [64], P('group'), may hold values from 2 to 2048, as said below
- queries: bfloat16 [320, 16384], P('group'), may hold values from -64 to 64
Outputs:
- attended: bfloat16 [320, 16384], P('group', 'dev')
- migrated_cache: bfloat16 [256, 8192, 256], P('group', 'dev')
- migrated_scale: bfloat16 [256, 8192, 2], P('group', 'dev')
The draws below stay inside these ranges and needn't reach their ends.
Inputs may be any that keep to these rules, and one draw needn't show every extreme that they name: `dest_group`: the 8 requests of one group send at most 1 to any one decode group, and one decode group receives at most 16 requests; both bounds are reached in every draw. `req_lengths`: some request has length 1024. `res_lengths`: some resident row has length 2048.
All inputs are finite; a program needn't handle non-finite values.
Results may differ from the reference program's by a relative error of at most 0.006.
Values may be sent and summed in bfloat16 or wider, within the bound.
A program may use at most 64 MiB of HBM per device.

```python
import math
import jax
import jax.numpy as jnp
from jax import lax

KVH = 8
HD = 128
QPK = 16
PAGE = 8
SLICE = 32
REQ = 8
RES = 4
GROUPS = 16
DEVS = 32
SPLIT = 4
SUB = 8
MAXLEN = 1024
RLEN = 2048
SEND_MOST = 1
CAP = 16
POOL = 32
REQUESTS = 128
RES_ROWS = 64
ROWS = 320
SLOTS = 256


def draw_dest_group(key, part):
    key = jax.random.fold_in(key, 1)
    busy_key, order_key, label_key, shuffle_key = jax.random.split(key, 4)
    busiest = jax.random.randint(busy_key, (), 0, GROUPS)
    sender_order = jax.random.permutation(order_key, GROUPS)
    sender_rank = jnp.argsort(sender_order)
    hot_count = jnp.where(sender_rank < CAP // SEND_MOST, SEND_MOST, 0)
    labels = jax.random.permutation(label_key, GROUPS - 1)
    request_slot = jnp.arange(REQ)[None, :]
    sender_ids = jnp.arange(GROUPS)[:, None]
    spread_label = labels[(sender_ids + request_slot - hot_count[:, None]) % (GROUPS - 1)]
    target = jnp.where(request_slot < hot_count[:, None], busiest, (busiest + 1 + spread_label) % GROUPS)
    shuffle = jax.vmap(lambda each_key: jax.random.permutation(each_key, REQ))(jax.random.split(shuffle_key, GROUPS))
    placement = jnp.argsort(shuffle, axis=1)
    result = jnp.take_along_axis(target, placement, axis=1)
    return result.reshape(REQUESTS).astype(jnp.int32)


def draw_req_lengths(key, part):
    key = jax.random.fold_in(key, 2)
    length_key, top_key = jax.random.split(key)
    values = jax.random.randint(length_key, (REQUESTS,), 1, MAXLEN + 1)
    longest = jax.random.randint(top_key, (), 0, REQUESTS)
    return jnp.where(jnp.arange(REQUESTS) == longest, MAXLEN, values).astype(jnp.int32)


def draw_res_lengths(key, part):
    key = jax.random.fold_in(key, 3)
    length_key, top_key = jax.random.split(key)
    values = jax.random.randint(length_key, (RES_ROWS,), 2, RLEN + 1)
    longest = jax.random.randint(top_key, (), 0, RES_ROWS)
    return jnp.where(jnp.arange(RES_ROWS) == longest, RLEN, values).astype(jnp.int32)


def draw_resident_kv(key, part):
    key = jax.random.fold_in(key, 4)
    values = jnp.clip(jax.random.normal(key, (RES_ROWS, KVH, RLEN, 2 * HD)), -6.0, 6.0)
    return values.reshape(RES_ROWS, KVH * RLEN, 2 * HD).astype(jnp.bfloat16)


def draw_resident_scale(key, part):
    key = jax.random.fold_in(key, 5)
    values = jnp.exp(jax.random.uniform(key, (RES_ROWS, KVH, RLEN, 2), jnp.float32, math.log(0.5), math.log(2.0)))
    return values.reshape(RES_ROWS, KVH * RLEN, 2).astype(jnp.bfloat16)


def draw_queries(key, part):
    key = jax.random.fold_in(key, 6)
    values = jnp.clip(jax.random.normal(key, (GROUPS, RES + CAP, KVH, QPK, HD)), -6.0, 6.0)
    return values.reshape(ROWS, KVH * QPK * HD).astype(jnp.bfloat16)


def level_of(own_key, extent, cuts, least, high):
    def one(position, shards_of):
        heights = jax.random.uniform(jax.random.fold_in(jax.random.fold_in(own_key, 6), position), (shards_of,), jnp.float32, least / len(cuts), high / len(cuts))
        return jnp.repeat(jnp.exp(heights), extent[position] // shards_of).reshape((-1,) + (1,) * (len(extent) - position - 1))

    loudness = one(*cuts[0])
    for cut in cuts[1:]:
        loudness = loudness * one(*cut)
    return loudness


def scatter_about(rng, dims, scale, most, cuts=(), kind=jnp.bfloat16):
    factor_of = level_of(rng, dims, cuts, -0.22, 0.18) if cuts else 1.0
    drawn = jax.random.normal(rng, dims, jnp.float32) * scale * factor_of
    return jnp.minimum(jnp.maximum(drawn, -most), most).astype(kind)


def setup_inputs(seed: int = 0) -> dict:
    key_of = jax.random.split(jax.random.key(seed), 9)
    return {
        "prefill_pool": scatter_about(key_of[0], (POOL * GROUPS, DEVS * PAGE, 2 * KVH * HD), 1.0, 6.0, ((0, 16), (1, 32))),
        "page_table": jax.vmap(lambda own: jax.random.permutation(own, POOL))(jax.random.split(key_of[1], GROUPS * DEVS)).reshape((GROUPS, DEVS, POOL)).astype(jnp.int32),
        "req_lengths": draw_req_lengths(jax.random.fold_in(key_of[8], 71), 0),
        "dest_group": draw_dest_group(jax.random.fold_in(key_of[8], 71), 0),
        "resident_kv": draw_resident_kv(jax.random.fold_in(key_of[8], 71), 0),
        "resident_scale": draw_resident_scale(jax.random.fold_in(key_of[8], 71), 0),
        "res_lengths": draw_res_lengths(jax.random.fold_in(key_of[8], 71), 0),
        "queries": draw_queries(jax.random.fold_in(key_of[8], 71), 0),
    }


tiny_amount = 1e-06
largest_level = 448.0

def quantize_rows(token_cache):
    peak_value = lax.optimization_barrier(jnp.max(jnp.abs(token_cache), axis=-1))
    block_scale = ((peak_value + tiny_amount) / largest_level).astype(jnp.bfloat16)
    stored = (token_cache / block_scale.astype(jnp.float32)[..., None]).astype(jnp.bfloat16)
    return (stored, block_scale)

def attend_rows(query_rows, key_rows, key_scale, value_rows, value_scale, positions, lengths):
    row_total = query_rows.shape[0]
    scores = jnp.einsum('rhqe,rhne->rhqn', query_rows.astype(jnp.float32), key_rows.astype(jnp.float32))
    scores = scores * key_scale.astype(jnp.float32)[:, :, None, :] / math.sqrt(HD)
    usable = (positions[None, :] < lengths[:, None])[:, None, None, :]
    highest = lax.optimization_barrier(jnp.max(jnp.where(usable, scores, -1e+30), axis=-1, keepdims=True))
    raised = jnp.where(usable, jnp.exp(scores - highest), 0.0)
    weight_sum = lax.optimization_barrier(jnp.sum(raised, axis=-1))
    weight = (raised * value_scale.astype(jnp.float32)[:, :, None, :]).astype(jnp.bfloat16)
    numerator = jnp.einsum('rhqn,rhne->rhqe', weight.astype(jnp.float32), value_rows.astype(jnp.float32))
    result = numerator / jnp.maximum(weight_sum, 1.0)[..., None]
    return result.astype(jnp.bfloat16).reshape(row_total, KVH * QPK * HD)

def reference(prefill_pool, page_table, req_lengths, dest_group, resident_kv, resident_scale, res_lengths, queries):
    pages_dev = SLICE // PAGE
    pool = prefill_pool.reshape(GROUPS, POOL, DEVS, PAGE, 2 * KVH * HD)
    request_ids = jnp.arange(REQUESTS, dtype=jnp.int32)
    same_dest = dest_group[None, :] == dest_group[:, None]
    earlier = request_ids[None, :] < request_ids[:, None]
    queue_rank = lax.optimization_barrier(jnp.sum(jnp.where(same_dest & earlier, 1, 0), axis=1)).astype(jnp.int32)
    res_cache = resident_kv.reshape(GROUPS, RES, KVH, RLEN, 2 * HD)
    res_scales = resident_scale.reshape(GROUPS, RES, KVH, RLEN, 2)
    res_used = res_lengths.reshape(GROUPS, RES)
    query_all = queries.reshape(GROUPS, RES + CAP, KVH, QPK, HD)

    def one_group(group_id):
        matches = (dest_group[None, :] == group_id) & (queue_rank[None, :] == jnp.arange(CAP, dtype=jnp.int32)[:, None])
        present = jnp.any(matches, axis=1)
        chosen = lax.optimization_barrier(jnp.sum(jnp.where(matches, request_ids[None, :], 0), axis=1)).astype(jnp.int32)
        source_group = (chosen // REQ).astype(jnp.int32)
        source_local = (chosen % REQ).astype(jnp.int32)
        table_rows = page_table[source_group]
        page_index = source_local[:, None] * pages_dev + jnp.arange(pages_dev, dtype=jnp.int32)[None, :]
        page_index = jnp.broadcast_to(page_index[:, None, :], (CAP, DEVS, pages_dev))
        slot_index = jnp.take_along_axis(table_rows, page_index, axis=2)
        token_cache = pool[source_group[:, None, None], slot_index, jnp.arange(DEVS, dtype=jnp.int32)[None, :, None]]
        token_cache = token_cache.reshape(CAP, MAXLEN, 2, KVH, HD).astype(jnp.float32)
        stored, block_scale = quantize_rows(token_cache)
        slot_length = jnp.where(present, req_lengths[chosen], 0).astype(jnp.int32)
        cache_layout = stored.reshape(CAP, DEVS, SPLIT, SUB, 2, KVH, HD)
        cache_layout = jnp.transpose(cache_layout, (0, 5, 2, 1, 3, 4, 6)).reshape(CAP, KVH * MAXLEN, 2 * HD)
        scale_layout = block_scale.reshape(CAP, DEVS, SPLIT, SUB, 2, KVH)
        scale_layout = jnp.transpose(scale_layout, (0, 5, 2, 1, 3, 4)).reshape(CAP, KVH * MAXLEN, 2)
        empty_value = jnp.zeros((), dtype=stored.dtype)
        migrated_cache = jnp.where(present[:, None, None], cache_layout, empty_value)
        migrated_scale = jnp.where(present[:, None, None], scale_layout, empty_value)
        key_rows = jnp.transpose(stored[:, :, 0], (0, 2, 1, 3))
        value_rows = jnp.transpose(stored[:, :, 1], (0, 2, 1, 3))
        key_scale = jnp.transpose(block_scale[:, :, 0], (0, 2, 1))
        value_scale = jnp.transpose(block_scale[:, :, 1], (0, 2, 1))
        migrated = attend_rows(query_all[group_id, RES:], key_rows, key_scale, value_rows, value_scale, jnp.arange(MAXLEN, dtype=jnp.int32), slot_length)
        own_cache = res_cache[group_id]
        own_scale = res_scales[group_id]
        resident = attend_rows(query_all[group_id, :RES], own_cache[..., :HD], own_scale[..., 0], own_cache[..., HD:], own_scale[..., 1], jnp.arange(RLEN, dtype=jnp.int32), res_used[group_id])
        return (jnp.concatenate([resident, migrated], axis=0), migrated_cache, migrated_scale)
    outputs, caches, scales = lax.map(one_group, jnp.arange(GROUPS, dtype=jnp.int32))
    return (outputs.reshape(ROWS, KVH * QPK * HD), caches.reshape(SLOTS, KVH * MAXLEN, 2 * HD), scales.reshape(SLOTS, KVH * MAXLEN, 2))
```

```python
import functools
import math

import jax
import jax.numpy as jnp
from jax import lax
from jax.experimental import pallas as pl
from jax.experimental.pallas import tpu as pltpu
from jax.sharding import PartitionSpec as P

KVH = 8
HD = 128
QPK = 16
PAGE = 8
GROUPS = 16
DEVS = 32
SPLIT = 4
REQ = 8
RES = 4
CAP = 16
ROWS = RES + CAP
TOKENS = DEVS * PAGE
RES_TOKENS = 512
SHARE = QPK // SPLIT

TINY = 1e-06
LEVEL = 448.0
NONE = -1e30
MESH = pl.DeviceIdType.MESH

CHUNKS = ((0, 1, 7), (2, 6), (3, 5), (4,))
COUNTS = tuple(4 * len(chunk) for chunk in CHUNKS)


def attend(query, keys, values, key_scale, value_scale, usable):
    scores = lax.dot_general(
        query, keys, (((1,), (1,)), ((), ())), preferred_element_type=jnp.float32
    )
    scores = scores * (key_scale * (1.0 / math.sqrt(HD)))
    highest = jnp.max(jnp.where(usable, scores, NONE), axis=1, keepdims=True)
    raised = jnp.where(usable, jnp.exp(scores - highest), 0.0)
    weight_sum = jnp.sum(raised, axis=1, keepdims=True)
    weight = (raised * value_scale).astype(jnp.bfloat16)
    numerator = jnp.dot(weight, values, preferred_element_type=jnp.float32)
    return numerator, highest, weight_sum


def kernel(
    table_ref,
    dest_ref,
    length_ref,
    res_length_ref,
    pool_ref,
    query_ref,
    res_kv_ref,
    res_scale_ref,
    attended_ref,
    cache_out_ref,
    scale_out_ref,
    send1,
    got1_0,
    got1_1,
    got1_2,
    got1_3,
    send2_0,
    send2_1,
    send2_2,
    send2_3,
    got2_0,
    got2_1,
    got2_2,
    got2_3,
    meta_send,
    meta_got,
    meta_smem,
    slot_source,
    slot_length,
    cache,
    scales,
    part_send,
    part_got,
    stat_send,
    stat_got,
    send1_sem,
    got1_sem,
    send2_sem,
    got2_sem,
    meta_sem,
    part_sem,
    stat_sem,
    local_sem,
):
    got1 = (got1_0, got1_1, got1_2, got1_3)
    send2 = (send2_0, send2_1, send2_2, send2_3)
    got2 = (got2_0, got2_1, got2_2, got2_3)
    group = lax.axis_index("group")
    dev = lax.axis_index("dev")
    x_hi = dev // 16
    pair = (dev % 16) // 2
    parity = dev % 2
    head = dev // SPLIT
    part = dev % SPLIT

    def peer_dev(offset, dx, dp):
        return (
            lax.rem(x_hi + dx, 2) * 16 + lax.rem(pair + offset, 8) * 2 + lax.rem(parity + dp, 2)
        )

    def request_for(target):
        picked = jnp.int32(0)
        for j in range(REQ):
            picked = jnp.where(dest_ref[j] == target, j, picked)
        return picked

    def length_for(target):
        picked = jnp.int32(0)
        for j in range(REQ):
            picked = jnp.where(dest_ref[j] == target, length_ref[j], picked)
        return picked

    barrier = pltpu.get_barrier_semaphore()
    dev_peers = [
        (offset, dx, dp)
        for chunk in CHUNKS
        for offset in chunk
        for dx in range(2)
        for dp in range(2)
        if (offset, dx, dp) != (0, 0, 0)
    ]
    for peer in dev_peers:
        pl.semaphore_signal(
            barrier, inc=1, device_id=(group, peer_dev(*peer)), device_id_type=MESH
        )

    @pl.loop(1, GROUPS)
    def _(k):
        pl.semaphore_signal(
            barrier, inc=1, device_id=(lax.rem(group + k, GROUPS), dev), device_id_type=MESH
        )

    @pl.loop(0, REQ)
    def _(j):
        for s in range(SPLIT):
            page = pool_ref[table_ref[j * SPLIT + s]].astype(jnp.float32)
            for h in range(KVH):
                block = jnp.concatenate(
                    [
                        page[:, h * HD : (h + 1) * HD],
                        page[:, (KVH + h) * HD : (KVH + h + 1) * HD],
                    ],
                    axis=0,
                )
                send1[h * SPLIT + s, j] = block.astype(jnp.bfloat16)

    @pl.loop(0, GROUPS)
    def _(g):
        meta_send[g] = jnp.full((1, 128), length_for(g), jnp.int32)

    pl.semaphore_wait(barrier, len(dev_peers) + GROUPS - 1)

    for c, chunk in enumerate(CHUNKS):
        for offset in chunk:
            for dx in range(2):
                for dp in range(2):
                    if (offset, dx, dp) == (0, 0, 0):
                        continue
                    to = peer_dev(offset, dx, dp)
                    place = chunk.index((8 - offset) % 8) * 4 + x_hi * 2 + parity
                    pltpu.make_async_remote_copy(
                        src_ref=send1.at[to],
                        dst_ref=got1[c].at[place],
                        send_sem=send1_sem,
                        recv_sem=got1_sem.at[c],
                        device_id=(group, to),
                        device_id_type=MESH,
                    ).start()

    @pl.loop(1, GROUPS)
    def _(k):
        to = lax.rem(group + k, GROUPS)
        pltpu.make_async_remote_copy(
            src_ref=meta_send.at[to],
            dst_ref=meta_got.at[group],
            send_sem=meta_sem.at[0],
            recv_sem=meta_sem.at[1],
            device_id=(to, dev),
            device_id_type=MESH,
        ).start()

    got1[0][x_hi * 2 + parity] = send1[dev]
    meta_got[group] = meta_send[group]

    lane16 = lax.broadcasted_iota(jnp.int32, (QPK, 128), 1)
    stat_highest = jnp.zeros((QPK, 128), jnp.float32)
    stat_sum = jnp.zeros((QPK, 128), jnp.float32)

    def keep(row, numerator, highest, weight_sum, stat_highest, stat_sum):
        for s in range(SPLIT):
            part_send[s, row] = numerator[s * SHARE : (s + 1) * SHARE]
        here = lane16 == row
        return jnp.where(here, highest, stat_highest), jnp.where(here, weight_sum, stat_sum)

    res_position = part * RES_TOKENS + lax.broadcasted_iota(jnp.int32, (QPK, RES_TOKENS), 1)
    for r in range(RES):
        row_scale = res_scale_ref[r].astype(jnp.float32)
        found = attend(
            query_ref[r],
            res_kv_ref[r, :, :HD],
            res_kv_ref[r, :, HD:],
            row_scale[0:1],
            row_scale[1:2],
            res_position < res_length_ref[r],
        )
        stat_highest, stat_sum = keep(r, *found, stat_highest, stat_sum)

    def forward(c):
        count = COUNTS[c]
        taken = count - 1 if c == 0 else count
        arrived = got1[c].at[pl.ds(0, taken)]
        pltpu.make_async_copy(arrived, arrived, got1_sem.at[c]).wait()
        got2[c][group] = got1[c][:, request_for(group)]

        @pl.loop(1, GROUPS)
        def _(k):
            to = lax.rem(group + k, GROUPS)
            send2[c][to] = got1[c][:, request_for(to)]
            pltpu.make_async_remote_copy(
                src_ref=send2[c].at[to],
                dst_ref=got2[c].at[group],
                send_sem=send2_sem.at[c],
                recv_sem=got2_sem.at[c],
                device_id=(to, dev),
                device_id_type=MESH,
            ).start()

    lane_rows = lax.broadcasted_iota(jnp.int32, (16, 128), 1)

    def store(c):
        count = COUNTS[c]
        others = got2[c].at[pl.ds(0, GROUPS - 1)]
        pltpu.make_async_copy(others, others, got2_sem.at[c]).wait()

        @pl.loop(0, CAP)
        def _(slot):
            present = slot_length[slot] > 0
            block = got2[c][slot_source[slot]].astype(jnp.float32)
            block = jnp.where(present, block, 0.0)
            peak = jnp.max(jnp.abs(block), axis=2, keepdims=True)
            scale = ((peak + TINY) / LEVEL).astype(jnp.bfloat16).astype(jnp.float32)
            stored = block * (1.0 / scale)
            scale = jnp.broadcast_to(jnp.where(present, scale, 0.0), block.shape)
            for p, offset in enumerate(CHUNKS[c]):
                at_pair = lax.rem(pair + offset, 8)
                for x in range(2):
                    at = pl.ds(pl.multiple_of((x * 16 + at_pair * 2) * PAGE, 16), 16)
                    n = p * 4 + x * 2
                    for kind in range(2):
                        rows = slice(kind * PAGE, (kind + 1) * PAGE)
                        both = jnp.concatenate([stored[n, rows], stored[n + 1, rows]], axis=0)
                        cache[slot, at, kind * HD : (kind + 1) * HD] = both.astype(jnp.bfloat16)
                    key_scale = jnp.concatenate([scale[n, :PAGE], scale[n + 1, :PAGE]], axis=0)
                    value_scale = jnp.concatenate([scale[n, PAGE:], scale[n + 1, PAGE:]], axis=0)
                    scales[slot, at] = jnp.where(lane_rows == 0, key_scale, value_scale).astype(
                        jnp.bfloat16
                    )

    forward(0)
    forward(1)

    metas = meta_got.at[pl.ds(0, GROUPS - 1)]
    pltpu.make_async_copy(metas, metas, meta_sem.at[1]).wait()
    pltpu.make_async_copy(meta_got, meta_smem, local_sem.at[0]).start()
    pltpu.make_async_copy(meta_got, meta_smem, local_sem.at[0]).wait()

    @pl.loop(0, CAP)
    def _(slot):
        source = jnp.int32(0)
        length = jnp.int32(0)
        rank = jnp.int32(0)
        for g in range(GROUPS):
            this_length = meta_smem[g, 0, 0]
            here = jnp.logical_and(this_length > 0, rank == slot)
            source = jnp.where(here, g, source)
            length = jnp.where(here, this_length, length)
            rank = rank + jnp.where(this_length > 0, 1, 0)
        slot_source[slot] = source
        slot_length[slot] = length

    store(0)
    forward(2)
    store(1)
    forward(3)
    store(2)
    store(3)

    cache_copy = pltpu.make_async_copy(cache, cache_out_ref, local_sem.at[1])
    cache_copy.start()

    index = lax.broadcasted_iota(jnp.int32, (QPK, TOKENS), 1)
    position = (index // PAGE) * (SPLIT * PAGE) + part * PAGE + index % PAGE
    row16 = lax.broadcasted_iota(jnp.int32, (QPK, 128), 0)
    pick = jnp.where(lane16 == row16 // PAGE, 1.0, 0.0).astype(jnp.bfloat16)

    def one_slot(slot, stats):
        rows = lax.dot_general(
            pick, scales[slot], (((1,), (1,)), ((), ())), preferred_element_type=jnp.float32
        )
        key_scale = rows[0:1]
        value_scale = rows[PAGE : PAGE + 1]
        scale_out_ref[slot, 0:1, :] = key_scale.astype(jnp.bfloat16)
        scale_out_ref[slot, 1:2, :] = value_scale.astype(jnp.bfloat16)
        found = attend(
            query_ref[RES + slot],
            cache[slot, :, :HD],
            cache[slot, :, HD:],
            key_scale,
            value_scale,
            position < slot_length[slot],
        )
        return keep(RES + slot, *found, *stats)

    def four_slots(i, stats):
        for k in range(4):
            stats = one_slot(i * 4 + k, stats)
        return stats

    stat_highest, stat_sum = lax.fori_loop(0, CAP // 4, four_slots, (stat_highest, stat_sum))
    for s in range(SPLIT):
        stat_send[s, :SHARE] = stat_highest[s * SHARE : (s + 1) * SHARE]
        stat_send[s, SHARE:] = stat_sum[s * SHARE : (s + 1) * SHARE]

    for k in range(1, SPLIT):
        s = lax.rem(part + k, SPLIT)
        to = (group, head * SPLIT + s)
        pltpu.make_async_remote_copy(
            src_ref=stat_send.at[s],
            dst_ref=stat_got.at[part],
            send_sem=stat_sem.at[0],
            recv_sem=stat_sem.at[1],
            device_id=to,
            device_id_type=MESH,
        ).start()
        pltpu.make_async_remote_copy(
            src_ref=part_send.at[s],
            dst_ref=part_got.at[part],
            send_sem=part_sem.at[0],
            recv_sem=part_sem.at[1],
            device_id=to,
            device_id_type=MESH,
        ).start()
    stat_got[part] = stat_send[part]
    part_got[part] = part_send[part]
    three_stats = stat_got.at[pl.ds(0, SPLIT - 1)]
    three_parts = part_got.at[pl.ds(0, SPLIT - 1)]
    pltpu.make_async_copy(three_stats, three_stats, stat_sem.at[1]).wait()
    highest = [stat_got[s, :SHARE] for s in range(SPLIT)]
    top = functools.reduce(jnp.maximum, highest)
    factors = [jnp.exp(each - top) for each in highest]
    total = functools.reduce(
        jnp.add, [stat_got[s, SHARE:] * factors[s] for s in range(SPLIT)]
    )
    total = jnp.maximum(total, 1.0)
    factors = [each / total for each in factors]
    pltpu.make_async_copy(three_parts, three_parts, part_sem.at[1]).wait()
    for r in range(ROWS):
        merged = functools.reduce(
            jnp.add, [part_got[s, r] * factors[s][:, r : r + 1] for s in range(SPLIT)]
        )
        part_send_row = merged
        for q in range(SHARE):
            attended_ref[r : r + 1, q * HD : (q + 1) * HD] = part_send_row[q : q + 1]

    sent = send1.at[pl.ds(0, DEVS - 1)]
    pltpu.make_async_copy(sent, sent, send1_sem).wait()
    for c in range(len(CHUNKS)):
        sent = send2[c].at[pl.ds(0, GROUPS - 1)]
        pltpu.make_async_copy(sent, sent, send2_sem.at[c]).wait()
    sent = meta_send.at[pl.ds(0, GROUPS - 1)]
    pltpu.make_async_copy(sent, sent, meta_sem.at[0]).wait()
    sent = stat_send.at[pl.ds(0, SPLIT - 1)]
    pltpu.make_async_copy(sent, sent, stat_sem.at[0]).wait()
    sent = part_send.at[pl.ds(0, SPLIT - 1)]
    pltpu.make_async_copy(sent, sent, part_sem.at[0]).wait()
    cache_copy.wait()


def body(
    prefill_pool,
    page_table,
    req_lengths,
    dest_group,
    resident_kv,
    resident_scale,
    res_lengths,
    queries,
):
    head = lax.axis_index("dev") // SPLIT
    my_queries = lax.dynamic_slice_in_dim(queries, head * (QPK * HD), QPK * HD, 1)
    my_queries = my_queries.reshape(ROWS, QPK, HD)
    smem = pl.BlockSpec(memory_space=pltpu.SMEM)
    vmem = pl.BlockSpec(memory_space=pltpu.VMEM)
    anywhere = pl.BlockSpec(memory_space=pl.ANY)
    bf16 = jnp.bfloat16
    attended, migrated_cache, migrated_scale = pl.pallas_call(
        kernel,
        out_shape=(
            jax.ShapeDtypeStruct((ROWS, SHARE * HD), jnp.float32),
            jax.ShapeDtypeStruct((CAP, TOKENS, 2 * HD), bf16),
            jax.ShapeDtypeStruct((CAP, 2, TOKENS), bf16),
        ),
        in_specs=[smem] * 4 + [vmem] * 4,
        out_specs=(vmem, anywhere, vmem),
        scratch_shapes=[
            pltpu.VMEM((DEVS, REQ, 2 * PAGE, HD), bf16),
            *[pltpu.VMEM((n, REQ, 2 * PAGE, HD), bf16) for n in COUNTS],
            *[pltpu.VMEM((GROUPS, n, 2 * PAGE, HD), bf16) for n in COUNTS],
            *[pltpu.VMEM((GROUPS, n, 2 * PAGE, HD), bf16) for n in COUNTS],
            pltpu.VMEM((GROUPS, 1, 128), jnp.int32),
            pltpu.VMEM((GROUPS, 1, 128), jnp.int32),
            pltpu.SMEM((GROUPS, 1, 128), jnp.int32),
            pltpu.SMEM((CAP,), jnp.int32),
            pltpu.SMEM((CAP,), jnp.int32),
            pltpu.VMEM((CAP, TOKENS, 2 * HD), bf16),
            pltpu.VMEM((CAP, TOKENS, 128), bf16),
            pltpu.VMEM((SPLIT, ROWS, SHARE, HD), jnp.float32),
            pltpu.VMEM((SPLIT, ROWS, SHARE, HD), jnp.float32),
            pltpu.VMEM((SPLIT, 2 * SHARE, 128), jnp.float32),
            pltpu.VMEM((SPLIT, 2 * SHARE, 128), jnp.float32),
            pltpu.SemaphoreType.DMA,
            pltpu.SemaphoreType.DMA((len(CHUNKS),)),
            pltpu.SemaphoreType.DMA((len(CHUNKS),)),
            pltpu.SemaphoreType.DMA((len(CHUNKS),)),
            pltpu.SemaphoreType.DMA((2,)),
            pltpu.SemaphoreType.DMA((2,)),
            pltpu.SemaphoreType.DMA((2,)),
            pltpu.SemaphoreType.DMA((2,)),
        ],
        compiler_params=pltpu.CompilerParams(
            collective_id=0, has_side_effects=True, vmem_limit_bytes=48 * 2**20
        ),
        name="migrate_and_attend",
    )(
        page_table.reshape(-1),
        dest_group,
        req_lengths,
        res_lengths,
        prefill_pool,
        my_queries,
        resident_kv,
        jnp.swapaxes(resident_scale, 1, 2),
    )
    return attended.astype(bf16), migrated_cache, jnp.swapaxes(migrated_scale, 1, 2)


def solution(mesh):
    return jax.shard_map(
        body,
        mesh=mesh,
        in_specs=(
            P("group", "dev", None),
            P("group", "dev", None),
            P("group"),
            P("group"),
            P("group", "dev", None),
            P("group", "dev", None),
            P("group"),
            P("group", None),
        ),
        out_specs=(P("group", "dev"), P("group", "dev", None), P("group", "dev", None)),
        check_vma=False,
    )
```

```python
import functools
import math

import jax
import jax.numpy as jnp
from jax import lax
from jax.experimental import pallas as pl
from jax.experimental.pallas import tpu as pltpu
from jax.sharding import PartitionSpec as P

KVH = 8
HD = 128
QPK = 16
PAGE = 8
GROUPS = 16
DEVS = 32
SPLIT = 4
REQ = 8
RES = 4
CAP = 16
ROWS = RES + CAP
TOKENS = DEVS * PAGE
RES_TOKENS = 512
SHARE = QPK // SPLIT

TINY = 1e-06
LEVEL = 448.0
NONE = -1e30
MESH = pl.DeviceIdType.MESH

CHUNKS = ((0, 1, 7), (2, 6), (3, 5), (4,))
COUNTS = tuple(4 * len(chunk) for chunk in CHUNKS)
LATE = (2, 3)


def attend(queries, keys, values, scales, usable):
    count = len(queries)
    scores = [
        lax.dot_general(
            queries[i], keys[i], (((1,), (1,)), ((), ())), preferred_element_type=jnp.float32
        )
        for i in range(count)
    ]
    scores = [
        jnp.where(usable[i], scores[i] * (scales[i][0] * (1.0 / math.sqrt(HD))), NONE)
        for i in range(count)
    ]
    highest = [jnp.max(each, axis=1, keepdims=True) for each in scores]
    raised = [
        jnp.where(usable[i], jnp.exp(scores[i] - highest[i]), 0.0) for i in range(count)
    ]
    weight_sum = [jnp.sum(each, axis=1, keepdims=True) for each in raised]
    numerator = [
        jnp.dot(
            (raised[i] * scales[i][1]).astype(jnp.bfloat16),
            values[i],
            preferred_element_type=jnp.float32,
        )
        for i in range(count)
    ]
    return numerator, highest, weight_sum


def kernel(
    table_hbm,
    dest_hbm,
    length_hbm,
    res_length_hbm,
    pool_hbm,
    query_hbm,
    res_kv_hbm,
    res_scale_hbm,
    attended_out_ref,
    cache_out_ref,
    scale_out_ref,
    table_ref,
    dest_ref,
    length_ref,
    res_length_ref,
    pool_ref,
    query_in,
    res_kv_ref,
    res_scale_ref,
    query_ref,
    send1,
    got1_0,
    got1_1,
    got1_2,
    got1_3,
    send2_0,
    send2_1,
    send2_2,
    send2_3,
    got2_0,
    got2_1,
    got2_2,
    got2_3,
    meta_send,
    meta_got,
    meta_smem,
    picked,
    slot_source,
    slot_length,
    cache,
    scales,
    early_numerator,
    early_highest,
    early_sum,
    scale_rows_ref,
    merged_ref,
    attended_ref,
    part_send,
    part_got,
    stat_send,
    stat_got,
    send1_sem,
    got1_sem,
    send2_sem,
    got2_sem,
    meta_sem,
    part_sem,
    stat_sem,
    local_sem,
    cache_sem,
    in_sem,
):
    got1 = (got1_0, got1_1, got1_2, got1_3)
    send2 = (send2_0, send2_1, send2_2, send2_3)
    got2 = (got2_0, got2_1, got2_2, got2_3)
    group = lax.axis_index("group")
    dev = lax.axis_index("dev")
    x_hi = dev // 16
    pair = (dev % 16) // 2
    parity = dev % 2
    head = dev // SPLIT
    part = dev % SPLIT

    x_parts = (x_hi * 16, (1 - x_hi) * 16)
    pair_parts = [lax.rem(pair + k, 8) * 2 for k in range(8)]
    parities = (parity, 1 - parity)

    def peer_dev(offset, dx, dp):
        return x_parts[dx] + pair_parts[offset] + parities[dp]

    def request_for(target):
        picked = jnp.int32(0)
        for j in range(REQ):
            picked = jnp.where(dest_ref[j] == target, j, picked)
        return picked

    def length_for(target):
        picked = jnp.int32(0)
        for j in range(REQ):
            picked = jnp.where(dest_ref[j] == target, length_ref[j], picked)
        return picked

    loads = [
        pltpu.make_async_copy(source, target, in_sem.at[i])
        for i, (source, target) in enumerate(
            (
                (table_hbm, table_ref),
                (dest_hbm, dest_ref),
                (length_hbm, length_ref),
                (res_length_hbm, res_length_ref),
                (pool_hbm, pool_ref),
                (
                    query_hbm.at[:, pl.ds(pl.multiple_of(head * (QPK * HD), 128), QPK * HD)],
                    query_in,
                ),
                (res_kv_hbm, res_kv_ref),
                (res_scale_hbm, res_scale_ref),
            )
        )
    ]
    for load in loads:
        load.start()

    barrier = pltpu.get_barrier_semaphore()
    dev_peers = [
        (offset, dx, dp)
        for chunk in CHUNKS
        for offset in chunk
        for dx in range(2)
        for dp in range(2)
        if (offset, dx, dp) != (0, 0, 0)
    ]
    for peer in dev_peers:
        pl.semaphore_signal(
            barrier, inc=1, device_id=(group, peer_dev(*peer)), device_id_type=MESH
        )

    @pl.loop(1, GROUPS)
    def _(k):
        pl.semaphore_signal(
            barrier, inc=1, device_id=(lax.rem(group + k, GROUPS), dev), device_id_type=MESH
        )

    for load in loads[:5]:
        load.wait()

    @pl.loop(0, REQ)
    def _(j):
        for s in range(SPLIT):
            page = pool_ref[table_ref[0, 0, j * SPLIT + s]].astype(jnp.float32)
            for h in range(KVH):
                block = jnp.concatenate(
                    [
                        page[:, h * HD : (h + 1) * HD],
                        page[:, (KVH + h) * HD : (KVH + h + 1) * HD],
                    ],
                    axis=0,
                )
                send1[h * SPLIT + s, j] = block.astype(jnp.bfloat16)

    pl.semaphore_wait(barrier, len(dev_peers) + GROUPS - 1)

    for c, chunk in enumerate(CHUNKS):
        for offset in chunk:
            for dx in range(2):
                for dp in range(2):
                    if (offset, dx, dp) == (0, 0, 0):
                        continue
                    to = peer_dev(offset, dx, dp)
                    place = chunk.index((8 - offset) % 8) * 4 + x_hi * 2 + parity
                    pltpu.make_async_remote_copy(
                        src_ref=send1.at[to],
                        dst_ref=got1[c].at[place],
                        send_sem=send1_sem,
                        recv_sem=got1_sem.at[c],
                        device_id=(group, to),
                        device_id_type=MESH,
                    ).start()

    @pl.loop(0, GROUPS)
    def _(g):
        meta_send[g] = jnp.full((1, 128), length_for(g), jnp.int32)
        picked[g] = request_for(g)

    @pl.loop(1, GROUPS)
    def _(k):
        to = lax.rem(group + k, GROUPS)
        pltpu.make_async_remote_copy(
            src_ref=meta_send.at[to],
            dst_ref=meta_got.at[group],
            send_sem=meta_sem.at[0],
            recv_sem=meta_sem.at[1],
            device_id=(to, dev),
            device_id_type=MESH,
        ).start()

    got1[0][x_hi * 2 + parity] = send1[dev]
    meta_got[group] = meta_send[group]

    for load in loads[5:]:
        load.wait()
    heads = query_in[...].astype(jnp.float32)
    for q in range(QPK):
        query_ref[:, q, :] = heads[:, q * HD : (q + 1) * HD]
    lane16 = lax.broadcasted_iota(jnp.int32, (QPK, 128), 1)
    stat_highest = jnp.zeros((QPK, 128), jnp.float32)
    stat_sum = jnp.zeros((QPK, 128), jnp.float32)

    def keep(row, highest, weight_sum, stats):
        here = lane16 == row
        return jnp.where(here, highest, stats[0]), jnp.where(here, weight_sum, stats[1])

    def put(four, numerators):
        for s in range(SPLIT):
            share = [each[s * SHARE : (s + 1) * SHARE] for each in numerators]
            part_send[s, four * 16 : (four + 1) * 16] = jnp.concatenate(share, axis=0).astype(
                part_send.dtype
            )

    stats = (stat_highest, stat_sum)
    res_position = part * RES_TOKENS + lax.broadcasted_iota(jnp.int32, (QPK, RES_TOKENS), 1)
    row_scales = [res_scale_ref[r].astype(jnp.float32) for r in range(RES)]
    numerators, highest, weight_sum = attend(
        [query_ref[r].astype(jnp.bfloat16) for r in range(RES)],
        [res_kv_ref[r, :, :HD] for r in range(RES)],
        [res_kv_ref[r, :, HD:] for r in range(RES)],
        [(each[0:1], each[1:2]) for each in row_scales],
        [res_position < res_length_ref[r] for r in range(RES)],
    )
    for r in range(RES):
        stats = keep(r, highest[r], weight_sum[r], stats)
    put(0, numerators)

    def rows_of(c):
        places = []
        for offset in CHUNKS[c]:
            for x in range(2):
                places.append(pl.ds(pl.multiple_of((x * 16 * PAGE) + pair_parts[offset] * PAGE, 16), 16))
        return places

    late_rows = [at for c in LATE for at in rows_of(c)]

    @pl.loop(0, CAP)
    def _(slot):
        for at in late_rows:
            cache[slot, at, :] = jnp.zeros((16, 2 * HD), jnp.bfloat16)
            scales[slot, at, :] = jnp.zeros((16, 128), jnp.bfloat16)

    def forward(c):
        count = COUNTS[c]
        taken = count - 1 if c == 0 else count
        arrived = got1[c].at[pl.ds(0, taken)]
        pltpu.make_async_copy(arrived, arrived, got1_sem.at[c]).wait()
        got2[c][group] = got1[c][:, picked[group]]

        @pl.loop(0, 3)
        def _(third):
            targets = [lax.rem(group + third * 5 + k, GROUPS) for k in range(1, 6)]
            for to in targets:
                send2[c][to] = got1[c][:, picked[to]]
            for to in targets:
                pltpu.make_async_remote_copy(
                    src_ref=send2[c].at[to],
                    dst_ref=got2[c].at[group],
                    send_sem=send2_sem.at[c],
                    recv_sem=got2_sem.at[c],
                    device_id=(to, dev),
                    device_id_type=MESH,
                ).start()

    lane_rows = lax.broadcasted_iota(jnp.int32, (16, 128), 1)

    def store(c):
        count = COUNTS[c]
        others = got2[c].at[pl.ds(0, GROUPS - 1)]
        pltpu.make_async_copy(others, others, got2_sem.at[c]).wait()

        places = rows_of(c)

        @pl.loop(0, CAP // 2)
        def _(two):
            for k in range(2):
                slot = two * 2 + k
                present = slot_length[slot] > 0
                block = got2[c][slot_source[slot]].astype(jnp.float32)
                block = jnp.where(present, block, 0.0)
                peak = jnp.max(jnp.abs(block), axis=2, keepdims=True)
                scale = ((peak + TINY) / LEVEL).astype(jnp.bfloat16).astype(jnp.float32)
                stored = block * (1.0 / scale)
                scale = jnp.broadcast_to(jnp.where(present, scale, 0.0), block.shape)
                for i, at in enumerate(places):
                    n = i * 2
                    for kind in range(2):
                        rows = slice(kind * PAGE, (kind + 1) * PAGE)
                        both = jnp.concatenate([stored[n, rows], stored[n + 1, rows]], axis=0)
                        cache[slot, at, kind * HD : (kind + 1) * HD] = both.astype(jnp.bfloat16)
                    key_scale = jnp.concatenate([scale[n, :PAGE], scale[n + 1, :PAGE]], axis=0)
                    value_scale = jnp.concatenate([scale[n, PAGE:], scale[n + 1, PAGE:]], axis=0)
                    scales[slot, at] = jnp.where(lane_rows == 0, key_scale, value_scale).astype(
                        jnp.bfloat16
                    )

        for at in places:
            pltpu.make_async_copy(
                cache.at[:, at, :], cache_out_ref.at[:, at, :], cache_sem
            ).start()

    forward(0)
    forward(1)

    metas = meta_got.at[pl.ds(0, GROUPS - 1)]
    pltpu.make_async_copy(metas, metas, meta_sem.at[1]).wait()
    pltpu.make_async_copy(meta_got, meta_smem, local_sem.at[0]).start()
    pltpu.make_async_copy(meta_got, meta_smem, local_sem.at[0]).wait()

    @pl.loop(0, CAP)
    def _(slot):
        source = jnp.int32(0)
        length = jnp.int32(0)
        rank = jnp.int32(0)
        for g in range(GROUPS):
            this_length = meta_smem[g, 0, 0]
            here = jnp.logical_and(this_length > 0, rank == slot)
            source = jnp.where(here, g, source)
            length = jnp.where(here, this_length, length)
            rank = rank + jnp.where(this_length > 0, 1, 0)
        slot_source[slot] = source
        slot_length[slot] = length

    row16 = lax.broadcasted_iota(jnp.int32, (QPK, 128), 0)
    pick = jnp.where(lane16 == row16 // PAGE, 1.0, 0.0).astype(jnp.bfloat16)

    def scale_rows(block):
        return lax.dot_general(
            pick, block, (((1,), (1,)), ((), ())), preferred_element_type=jnp.float32
        )

    def attend_early():
        index = lax.broadcasted_iota(jnp.int32, (QPK, TOKENS), 1)
        device = index // PAGE
        position = device * (SPLIT * PAGE) + part * PAGE + index % PAGE
        its_pair = (device % 16) // 2
        early = its_pair >= 0
        for c in LATE:
            for offset in CHUNKS[c]:
                early = jnp.logical_and(early, its_pair * 2 != pair_parts[offset])

        @pl.loop(0, CAP // 4)
        def _(four):
            slots = [four * 4 + k for k in range(4)]
            rows = [scale_rows(scales[slot]) for slot in slots]
            numerator, highest, weight_sum = attend(
                [query_ref[RES + slot].astype(jnp.bfloat16) for slot in slots],
                [cache[slot, :, :HD] for slot in slots],
                [cache[slot, :, HD:] for slot in slots],
                [(each[0:1], each[PAGE : PAGE + 1]) for each in rows],
                [jnp.logical_and(early, position < slot_length[slot]) for slot in slots],
            )
            for k, slot in enumerate(slots):
                early_numerator[slot] = numerator[k]
                early_highest[slot] = jnp.broadcast_to(highest[k], (QPK, 128))
                early_sum[slot] = jnp.broadcast_to(weight_sum[k], (QPK, 128))

    def attend_late(stats):
        wide = 16 * len(late_rows)
        index = lax.broadcasted_iota(jnp.int32, (QPK, wide), 1)
        device = jnp.zeros((QPK, wide), jnp.int32)
        n = 0
        for c in LATE:
            for offset in CHUNKS[c]:
                for x in range(2):
                    device = jnp.where(index // 16 == n, x * 16 + pair_parts[offset], device)
                    n += 1
        device = device + (index % 16) // PAGE
        position = device * (SPLIT * PAGE) + part * PAGE + index % PAGE
        for eight in range(CAP // 8):
            slots = [eight * 8 + k for k in range(8)]
            rows = [
                scale_rows(jnp.concatenate([scales[slot, at, :] for at in late_rows], axis=0))
                for slot in slots
            ]
            tokens = [
                jnp.concatenate([cache[slot, at, :] for at in late_rows], axis=0)
                for slot in slots
            ]
            numerator, highest, weight_sum = attend(
                [query_ref[RES + slot].astype(jnp.bfloat16) for slot in slots],
                [each[:, :HD] for each in tokens],
                [each[:, HD:] for each in tokens],
                [(each[0:1], each[PAGE : PAGE + 1]) for each in rows],
                [position < slot_length[slot] for slot in slots],
            )
            tops = [jnp.maximum(early_highest[slots[k]], highest[k]) for k in range(8)]
            early_factors = [jnp.exp(early_highest[slots[k]] - tops[k]) for k in range(8)]
            factors = [jnp.exp(highest[k] - tops[k]) for k in range(8)]
            numerators = [
                early_numerator[slots[k]] * early_factors[k] + numerator[k] * factors[k]
                for k in range(8)
            ]
            for k in range(8):
                total = early_sum[slots[k]] * early_factors[k] + weight_sum[k] * factors[k]
                stats = keep(RES + slots[k], tops[k], total, stats)
            put(1 + eight * 2, numerators[:4])
            put(2 + eight * 2, numerators[4:])
        return stats

    store(0)
    forward(2)
    store(1)
    forward(3)
    attend_early()
    store(2)
    store(3)
    stats = attend_late(stats)
    for s in range(SPLIT):
        stat_send[s, :SHARE] = stats[0][s * SHARE : (s + 1) * SHARE]
        stat_send[s, SHARE:] = stats[1][s * SHARE : (s + 1) * SHARE]

    for k in range(1, SPLIT):
        s = lax.rem(part + k, SPLIT)
        to = (group, head * SPLIT + s)
        pltpu.make_async_remote_copy(
            src_ref=stat_send.at[s],
            dst_ref=stat_got.at[part],
            send_sem=stat_sem.at[0],
            recv_sem=stat_sem.at[1],
            device_id=to,
            device_id_type=MESH,
        ).start()
        pltpu.make_async_remote_copy(
            src_ref=part_send.at[s],
            dst_ref=part_got.at[part],
            send_sem=part_sem.at[0],
            recv_sem=part_sem.at[1],
            device_id=to,
            device_id_type=MESH,
        ).start()
    stat_got[part] = stat_send[part]
    part_got[part] = part_send[part]

    @pl.loop(0, CAP // 4)
    def _(four):
        slots = [four * 4 + k for k in range(4)]
        rows = [scale_rows(scales[slot]).astype(jnp.bfloat16) for slot in slots]
        for k, slot in enumerate(slots):
            scale_rows_ref[slot, 0:1, :] = rows[k][0:1]
            scale_rows_ref[slot, 1:2, :] = rows[k][PAGE : PAGE + 1]

    scale_copy = pltpu.make_async_copy(scale_rows_ref, scale_out_ref, local_sem.at[2])
    scale_copy.start()

    three_stats = stat_got.at[pl.ds(0, SPLIT - 1)]
    three_parts = part_got.at[pl.ds(0, SPLIT - 1)]
    pltpu.make_async_copy(three_stats, three_stats, stat_sem.at[1]).wait()
    highest = [stat_got[s, :SHARE] for s in range(SPLIT)]
    top = functools.reduce(jnp.maximum, highest)
    factors = [jnp.exp(each - top) for each in highest]
    total = functools.reduce(jnp.add, [stat_got[s, SHARE:] * factors[s] for s in range(SPLIT)])
    total = jnp.maximum(total, 1.0)
    factors = [each / total for each in factors]
    pltpu.make_async_copy(three_parts, three_parts, part_sem.at[1]).wait()
    parts = [part_got[s].astype(jnp.float32) for s in range(SPLIT)]
    for r in range(ROWS):
        merged = functools.reduce(
            jnp.add,
            [
                parts[s][r * SHARE : (r + 1) * SHARE] * factors[s][:, r : r + 1]
                for s in range(SPLIT)
            ],
        )
        for q in range(SHARE):
            merged_ref[r : r + 1, q * HD : (q + 1) * HD] = merged[q : q + 1]
    attended_ref[...] = merged_ref[...].astype(jnp.bfloat16)
    attended_copy = pltpu.make_async_copy(attended_ref, attended_out_ref, local_sem.at[3])
    attended_copy.start()

    sent = send1.at[pl.ds(0, DEVS - 1)]
    pltpu.make_async_copy(sent, sent, send1_sem).wait()
    for c in range(len(CHUNKS)):
        sent = send2[c].at[pl.ds(0, GROUPS - 1)]
        pltpu.make_async_copy(sent, sent, send2_sem.at[c]).wait()
    sent = meta_send.at[pl.ds(0, GROUPS - 1)]
    pltpu.make_async_copy(sent, sent, meta_sem.at[0]).wait()
    sent = stat_send.at[pl.ds(0, SPLIT - 1)]
    pltpu.make_async_copy(sent, sent, stat_sem.at[0]).wait()
    sent = part_send.at[pl.ds(0, SPLIT - 1)]
    pltpu.make_async_copy(sent, sent, part_sem.at[0]).wait()
    pltpu.make_async_copy(cache, cache_out_ref, cache_sem).wait()
    scale_copy.wait()
    attended_copy.wait()


def copy_kernel(
    attended_in,
    cache_in,
    scale_in,
    attended_out,
    cache_out,
    scale_out,
    attended_held,
    cache_held,
    scale_held,
    in_sem,
    out_sem,
):
    pieces = [
        (cache_in.at[at], cache_held.at[at], cache_out.at[at])
        for at in (pl.ds(i * 2, 2) for i in range(CAP // 2))
    ]
    pieces.append((scale_in, scale_held, scale_out))
    pieces.append((attended_in, attended_held, attended_out))
    loads = [pltpu.make_async_copy(p[0], p[1], in_sem.at[i]) for i, p in enumerate(pieces)]
    stores = [pltpu.make_async_copy(p[1], p[2], out_sem.at[i]) for i, p in enumerate(pieces)]
    for load in loads:
        load.start()
    for load, store in zip(loads, stores):
        load.wait()
        store.start()
    for store in stores:
        store.wait()


def body(
    prefill_pool,
    page_table,
    req_lengths,
    dest_group,
    resident_kv,
    resident_scale,
    res_lengths,
    queries,
):
    hbm = pl.BlockSpec(memory_space=pltpu.HBM)
    bf16 = jnp.bfloat16
    out_shape = (
        jax.ShapeDtypeStruct((ROWS, SHARE * HD), bf16),
        jax.ShapeDtypeStruct((CAP, TOKENS, 2 * HD), bf16),
        jax.ShapeDtypeStruct((CAP, 2, TOKENS), bf16),
    )
    results = pl.pallas_call(
        kernel,
        out_shape=out_shape,
        in_specs=[hbm] * 8,
        out_specs=(hbm,) * 3,
        scratch_shapes=[
            pltpu.SMEM((1, 1, REQ * SPLIT), jnp.int32),
            pltpu.SMEM((REQ,), jnp.int32),
            pltpu.SMEM((REQ,), jnp.int32),
            pltpu.SMEM((RES,), jnp.int32),
            pltpu.VMEM((REQ * SPLIT, PAGE, 2 * KVH * HD), bf16),
            pltpu.VMEM((ROWS, QPK * HD), bf16),
            pltpu.VMEM((RES, RES_TOKENS, 2 * HD), bf16),
            pltpu.VMEM((RES, 2, RES_TOKENS), bf16),
            pltpu.VMEM((ROWS, QPK, HD), jnp.float32),
            pltpu.VMEM((DEVS, REQ, 2 * PAGE, HD), bf16),
            *[pltpu.VMEM((n, REQ, 2 * PAGE, HD), bf16) for n in COUNTS],
            *[pltpu.VMEM((GROUPS, n, 2 * PAGE, HD), bf16) for n in COUNTS],
            *[pltpu.VMEM((GROUPS, n, 2 * PAGE, HD), bf16) for n in COUNTS],
            pltpu.VMEM((GROUPS, 1, 128), jnp.int32),
            pltpu.VMEM((GROUPS, 1, 128), jnp.int32),
            pltpu.SMEM((GROUPS, 1, 128), jnp.int32),
            pltpu.SMEM((GROUPS,), jnp.int32),
            pltpu.SMEM((CAP,), jnp.int32),
            pltpu.SMEM((CAP,), jnp.int32),
            pltpu.VMEM((CAP, TOKENS, 2 * HD), bf16),
            pltpu.VMEM((CAP, TOKENS, 128), bf16),
            *[pltpu.VMEM((CAP, QPK, HD), jnp.float32)] * 3,
            pltpu.VMEM((CAP, 2, TOKENS), bf16),
            pltpu.VMEM((ROWS, SHARE * HD), jnp.float32),
            pltpu.VMEM((ROWS, SHARE * HD), bf16),
            pltpu.VMEM((SPLIT, ROWS * SHARE, HD), jnp.float32),
            pltpu.VMEM((SPLIT, ROWS * SHARE, HD), jnp.float32),
            pltpu.VMEM((SPLIT, 2 * SHARE, 128), jnp.float32),
            pltpu.VMEM((SPLIT, 2 * SHARE, 128), jnp.float32),
            pltpu.SemaphoreType.DMA,
            pltpu.SemaphoreType.DMA((len(CHUNKS),)),
            pltpu.SemaphoreType.DMA((len(CHUNKS),)),
            pltpu.SemaphoreType.DMA((len(CHUNKS),)),
            pltpu.SemaphoreType.DMA((2,)),
            pltpu.SemaphoreType.DMA((2,)),
            pltpu.SemaphoreType.DMA((2,)),
            pltpu.SemaphoreType.DMA((4,)),
            pltpu.SemaphoreType.DMA,
            pltpu.SemaphoreType.DMA((8,)),
        ],
        compiler_params=pltpu.CompilerParams(
            collective_id=0, has_side_effects=True, vmem_limit_bytes=62 * 2**20
        ),
        name="migrate_and_attend",
    )(
        page_table,
        dest_group,
        req_lengths,
        res_lengths,
        prefill_pool,
        queries,
        resident_kv,
        jnp.swapaxes(resident_scale, 1, 2),
    )
    attended, migrated_cache, migrated_scale = pl.pallas_call(
        copy_kernel,
        out_shape=out_shape,
        in_specs=[hbm] * 3,
        out_specs=(hbm,) * 3,
        scratch_shapes=[
            *[pltpu.VMEM(each.shape, each.dtype) for each in out_shape],
            pltpu.SemaphoreType.DMA((CAP // 2 + 2,)),
            pltpu.SemaphoreType.DMA((CAP // 2 + 2,)),
        ],
        compiler_params=pltpu.CompilerParams(vmem_limit_bytes=62 * 2**20),
        name="copy_results",
    )(*results)
    return attended, migrated_cache, jnp.swapaxes(migrated_scale, 1, 2)


def solution(mesh):
    return jax.shard_map(
        body,
        mesh=mesh,
        in_specs=(
            P("group", "dev", None),
            P("group", "dev", None),
            P("group"),
            P("group"),
            P("group", "dev", None),
            P("group", "dev", None),
            P("group"),
            P("group", None),
        ),
        out_specs=(P("group", "dev"), P("group", "dev", None), P("group", "dev", None)),
        check_vma=False,
    )
```

```python
import functools
import math

import jax
import jax.numpy as jnp
from jax import lax
from jax.experimental import pallas as pl
from jax.experimental.pallas import tpu as pltpu
from jax.sharding import PartitionSpec as P

KVH = 8
HD = 128
QPK = 16
PAGE = 8
GROUPS = 16
DEVS = 32
SPLIT = 4
REQ = 8
RES = 4
CAP = 16
ROWS = RES + CAP
TOKENS = DEVS * PAGE
RES_TOKENS = 512
SHARE = QPK // SPLIT

TINY = 1e-06
LEVEL = 448.0
NONE = -1e30
MESH = pl.DeviceIdType.MESH

CHUNKS = (
    ((0, 0), (0, 1), (1, 0), (1, 1), (7, 0), (7, 1)),
    ((2, 0), (2, 1), (6, 0), (6, 1)),
    ((3, 0), (3, 1), (5, 0), (5, 1)),
    ((4, 0),),
    ((4, 1),),
)
COUNTS = tuple(2 * len(chunk) for chunk in CHUNKS)
LATE = (2, 3, 4)


def attend(queries, keys, values, scales, usable):
    count = len(queries)
    scores = [
        lax.dot_general(
            queries[i], keys[i], (((1,), (1,)), ((), ())), preferred_element_type=jnp.float32
        )
        for i in range(count)
    ]
    scores = [
        jnp.where(usable[i], scores[i] * (scales[i][0] * (1.0 / math.sqrt(HD))), NONE)
        for i in range(count)
    ]
    highest = [jnp.max(each, axis=1, keepdims=True) for each in scores]
    raised = [
        jnp.where(usable[i], jnp.exp(scores[i] - highest[i]), 0.0) for i in range(count)
    ]
    weight_sum = [jnp.sum(each, axis=1, keepdims=True) for each in raised]
    numerator = [
        jnp.dot(
            (raised[i] * scales[i][1]).astype(jnp.bfloat16),
            values[i],
            preferred_element_type=jnp.float32,
        )
        for i in range(count)
    ]
    return numerator, highest, weight_sum


def kernel(
    table_hbm,
    dest_hbm,
    length_hbm,
    res_length_hbm,
    pool_hbm,
    query_hbm,
    res_kv_hbm,
    res_scale_hbm,
    attended_out_ref,
    cache_out_ref,
    scale_out_ref,
    table_ref,
    dest_ref,
    length_ref,
    res_length_ref,
    pool_ref,
    query_in,
    res_kv_ref,
    res_scale_ref,
    query_ref,
    send1,
    got1_0,
    got1_1,
    got1_2,
    got1_3,
    got1_4,
    send2_0,
    send2_1,
    send2_2,
    send2_3,
    send2_4,
    got2_0,
    got2_1,
    got2_2,
    got2_3,
    got2_4,
    meta_send,
    meta_got,
    meta_smem,
    picked,
    slot_source,
    slot_length,
    cache,
    scales,
    early_numerator,
    early_highest,
    early_sum,
    scale_rows_ref,
    merged_ref,
    attended_ref,
    part_send,
    part_got,
    stat_send,
    stat_got,
    send1_sem,
    got1_sem,
    send2_sem,
    got2_sem,
    meta_sem,
    part_sem,
    stat_sem,
    local_sem,
    cache_sem,
    in_sem,
    ready_sem,
):
    got1 = (got1_0, got1_1, got1_2, got1_3, got1_4)
    send2 = (send2_0, send2_1, send2_2, send2_3, send2_4)
    got2 = (got2_0, got2_1, got2_2, got2_3, got2_4)
    group = lax.axis_index("group")
    dev = lax.axis_index("dev")
    x_hi = dev // 16
    pair = (dev % 16) // 2
    parity = dev % 2
    head = dev // SPLIT
    part = dev % SPLIT

    x_parts = (x_hi * 16, (1 - x_hi) * 16)
    pair_parts = [lax.rem(pair + k, 8) * 2 for k in range(8)]
    parities = (parity, 1 - parity)

    def peer_dev(offset, dx, dp):
        return x_parts[dx] + pair_parts[offset] + parities[dp]

    def request_for(target):
        picked = jnp.int32(0)
        for j in range(REQ):
            picked = jnp.where(dest_ref[j] == target, j, picked)
        return picked

    def length_for(target):
        picked = jnp.int32(0)
        for j in range(REQ):
            picked = jnp.where(dest_ref[j] == target, length_ref[j], picked)
        return picked

    loads = [
        pltpu.make_async_copy(source, target, in_sem.at[i])
        for i, (source, target) in enumerate(
            (
                (pool_hbm, pool_ref),
                (table_hbm, table_ref),
                (dest_hbm, dest_ref),
                (length_hbm, length_ref),
                (res_length_hbm, res_length_ref),
                (
                    query_hbm.at[:, pl.ds(pl.multiple_of(head * (QPK * HD), 128), QPK * HD)],
                    query_in,
                ),
                (res_kv_hbm, res_kv_ref),
                (res_scale_hbm, res_scale_ref),
            )
        )
    ]
    for load in loads[:5]:
        load.start()

    barrier = pltpu.get_barrier_semaphore()
    near = [
        (offset, dx, dp)
        for offset, dx in CHUNKS[0]
        for dp in range(2)
        if (offset, dx, dp) != (0, 0, 0)
    ]
    for peer in near:
        pl.semaphore_signal(
            barrier, inc=1, device_id=(group, peer_dev(*peer)), device_id_type=MESH
        )

    @pl.loop(1, GROUPS)
    def _(k):
        pl.semaphore_signal(
            barrier, inc=1, device_id=(lax.rem(group + k, GROUPS), dev), device_id_type=MESH
        )

    for load in loads[:5]:
        load.wait()
    for load in loads[5:]:
        load.start()

    @pl.loop(0, REQ)
    def _(j):
        for s in range(SPLIT):
            page = pool_ref[table_ref[0, 0, j * SPLIT + s]].astype(jnp.float32)
            for h in range(KVH):
                block = jnp.concatenate(
                    [
                        page[:, h * HD : (h + 1) * HD],
                        page[:, (KVH + h) * HD : (KVH + h + 1) * HD],
                    ],
                    axis=0,
                )
                send1[h * SPLIT + s, j] = block.astype(jnp.bfloat16)

    pl.semaphore_wait(barrier, len(near) + GROUPS - 1)

    def start(c):
        for dp in range(2):
            for offset, dx in CHUNKS[c]:
                if (offset, dx, dp) == (0, 0, 0):
                    continue
                to = peer_dev(offset, dx, dp)
                place = CHUNKS[c].index(((8 - offset) % 8, dx)) * 2 + parity
                pltpu.make_async_remote_copy(
                    src_ref=send1.at[to],
                    dst_ref=got1[c].at[place],
                    send_sem=send1_sem,
                    recv_sem=got1_sem.at[c],
                    device_id=(group, to),
                    device_id_type=MESH,
                ).start()

    def round_over(i):
        for offset in (1, 7):
            pl.semaphore_signal(
                ready_sem.at[i],
                inc=1,
                device_id=(group, peer_dev(offset, 0, 0)),
                device_id_type=MESH,
            )

    def await_round(i):
        pl.semaphore_wait(ready_sem.at[i], 2)

    round_over(0)
    start(0)
    await_round(0)
    round_over(1)
    start(1)
    await_round(1)
    round_over(2)
    start(2)
    await_round(2)
    start(3)
    start(4)

    @pl.loop(0, GROUPS)
    def _(g):
        meta_send[g] = jnp.full((1, 128), length_for(g), jnp.int32)
        picked[g] = request_for(g)

    @pl.loop(1, GROUPS)
    def _(k):
        to = lax.rem(group + k, GROUPS)
        pltpu.make_async_remote_copy(
            src_ref=meta_send.at[to],
            dst_ref=meta_got.at[group],
            send_sem=meta_sem.at[0],
            recv_sem=meta_sem.at[1],
            device_id=(to, dev),
            device_id_type=MESH,
        ).start()

    got1[0][parity] = send1[dev]
    meta_got[group] = meta_send[group]

    for load in loads[5:]:
        load.wait()
    heads = query_in[...].astype(jnp.float32)
    for q in range(QPK):
        query_ref[:, q, :] = heads[:, q * HD : (q + 1) * HD]
    lane16 = lax.broadcasted_iota(jnp.int32, (QPK, 128), 1)
    stat_highest = jnp.zeros((QPK, 128), jnp.float32)
    stat_sum = jnp.zeros((QPK, 128), jnp.float32)

    def keep(row, highest, weight_sum, stats):
        here = lane16 == row
        return jnp.where(here, highest, stats[0]), jnp.where(here, weight_sum, stats[1])

    def put(four, numerators):
        for s in range(SPLIT):
            share = [each[s * SHARE : (s + 1) * SHARE] for each in numerators]
            part_send[s, four * 16 : (four + 1) * 16] = jnp.concatenate(share, axis=0).astype(
                part_send.dtype
            )

    stats = (stat_highest, stat_sum)
    res_position = part * RES_TOKENS + lax.broadcasted_iota(jnp.int32, (QPK, RES_TOKENS), 1)
    row_scales = [res_scale_ref[r].astype(jnp.float32) for r in range(RES)]
    numerators, highest, weight_sum = attend(
        [query_ref[r].astype(jnp.bfloat16) for r in range(RES)],
        [res_kv_ref[r, :, :HD] for r in range(RES)],
        [res_kv_ref[r, :, HD:] for r in range(RES)],
        [(each[0:1], each[1:2]) for each in row_scales],
        [res_position < res_length_ref[r] for r in range(RES)],
    )
    for r in range(RES):
        stats = keep(r, highest[r], weight_sum[r], stats)
    put(0, numerators)

    def send_parts(rows):
        for k in range(1, SPLIT):
            s = lax.rem(part + k, SPLIT)
            pltpu.make_async_remote_copy(
                src_ref=part_send.at[s, rows],
                dst_ref=part_got.at[part, rows],
                send_sem=part_sem.at[0],
                recv_sem=part_sem.at[1],
                device_id=(group, head * SPLIT + s),
                device_id_type=MESH,
            ).start()

    send_parts(pl.ds(0, RES * SHARE))

    def rows_of(c):
        return [
            pl.ds(pl.multiple_of((x_parts[dx] + pair_parts[offset]) * PAGE, 16), 16)
            for offset, dx in CHUNKS[c]
        ]

    late_rows = [at for c in LATE for at in rows_of(c)]

    @pl.loop(0, CAP)
    def _(slot):
        for at in late_rows:
            cache[slot, at, :] = jnp.zeros((16, 2 * HD), jnp.bfloat16)
            scales[slot, at, :] = jnp.zeros((16, 128), jnp.bfloat16)

    def forward(c):
        count = COUNTS[c]
        taken = count - 1 if c == 0 else count
        arrived = got1[c].at[pl.ds(0, taken)]
        pltpu.make_async_copy(arrived, arrived, got1_sem.at[c]).wait()
        got2[c][group] = got1[c][:, picked[group]]

        @pl.loop(0, 3)
        def _(third):
            targets = [lax.rem(group + third * 5 + k, GROUPS) for k in range(1, 6)]
            for to in targets:
                send2[c][to] = got1[c][:, picked[to]]
            for to in targets:
                pltpu.make_async_remote_copy(
                    src_ref=send2[c].at[to],
                    dst_ref=got2[c].at[group],
                    send_sem=send2_sem.at[c],
                    recv_sem=got2_sem.at[c],
                    device_id=(to, dev),
                    device_id_type=MESH,
                ).start()

    lane_rows = lax.broadcasted_iota(jnp.int32, (16, 128), 1)

    def store(c):
        count = COUNTS[c]
        others = got2[c].at[pl.ds(0, GROUPS - 1)]
        pltpu.make_async_copy(others, others, got2_sem.at[c]).wait()

        places = rows_of(c)

        @pl.loop(0, CAP // 2)
        def _(two):
            for k in range(2):
                slot = two * 2 + k
                present = slot_length[slot] > 0
                block = got2[c][slot_source[slot]].astype(jnp.float32)
                block = jnp.where(present, block, 0.0)
                peak = jnp.max(jnp.abs(block), axis=2, keepdims=True)
                scale = ((peak + TINY) / LEVEL).astype(jnp.bfloat16).astype(jnp.float32)
                stored = block * (1.0 / scale)
                scale = jnp.broadcast_to(jnp.where(present, scale, 0.0), block.shape)
                for i, at in enumerate(places):
                    n = i * 2
                    for kind in range(2):
                        rows = slice(kind * PAGE, (kind + 1) * PAGE)
                        both = jnp.concatenate([stored[n, rows], stored[n + 1, rows]], axis=0)
                        cache[slot, at, kind * HD : (kind + 1) * HD] = both.astype(jnp.bfloat16)
                    key_scale = jnp.concatenate([scale[n, :PAGE], scale[n + 1, :PAGE]], axis=0)
                    value_scale = jnp.concatenate([scale[n, PAGE:], scale[n + 1, PAGE:]], axis=0)
                    scales[slot, at] = jnp.where(lane_rows == 0, key_scale, value_scale).astype(
                        jnp.bfloat16
                    )

        for at in places:
            pltpu.make_async_copy(
                cache.at[:, at, :], cache_out_ref.at[:, at, :], cache_sem
            ).start()

    forward(0)
    forward(1)

    metas = meta_got.at[pl.ds(0, GROUPS - 1)]
    pltpu.make_async_copy(metas, metas, meta_sem.at[1]).wait()
    pltpu.make_async_copy(meta_got, meta_smem, local_sem.at[0]).start()
    pltpu.make_async_copy(meta_got, meta_smem, local_sem.at[0]).wait()

    @pl.loop(0, CAP)
    def _(slot):
        source = jnp.int32(0)
        length = jnp.int32(0)
        rank = jnp.int32(0)
        for g in range(GROUPS):
            this_length = meta_smem[g, 0, 0]
            here = jnp.logical_and(this_length > 0, rank == slot)
            source = jnp.where(here, g, source)
            length = jnp.where(here, this_length, length)
            rank = rank + jnp.where(this_length > 0, 1, 0)
        slot_source[slot] = source
        slot_length[slot] = length

    row16 = lax.broadcasted_iota(jnp.int32, (QPK, 128), 0)
    pick = jnp.where(lane16 == row16 // PAGE, 1.0, 0.0).astype(jnp.bfloat16)

    def scale_rows(block):
        return lax.dot_general(
            pick, block, (((1,), (1,)), ((), ())), preferred_element_type=jnp.float32
        )

    def attend_early():
        index = lax.broadcasted_iota(jnp.int32, (QPK, TOKENS), 1)
        device = index // PAGE
        position = device * (SPLIT * PAGE) + part * PAGE + index % PAGE
        its_pair = (device % 16) // 2
        early = its_pair >= 0
        for c in LATE:
            for offset, _ in CHUNKS[c]:
                early = jnp.logical_and(early, its_pair * 2 != pair_parts[offset])

        @pl.loop(0, CAP // 4)
        def _(four):
            slots = [four * 4 + k for k in range(4)]
            rows = [scale_rows(scales[slot]) for slot in slots]
            numerator, highest, weight_sum = attend(
                [query_ref[RES + slot].astype(jnp.bfloat16) for slot in slots],
                [cache[slot, :, :HD] for slot in slots],
                [cache[slot, :, HD:] for slot in slots],
                [(each[0:1], each[PAGE : PAGE + 1]) for each in rows],
                [jnp.logical_and(early, position < slot_length[slot]) for slot in slots],
            )
            for k, slot in enumerate(slots):
                early_numerator[slot] = numerator[k]
                early_highest[slot] = jnp.broadcast_to(highest[k], (QPK, 128))
                early_sum[slot] = jnp.broadcast_to(weight_sum[k], (QPK, 128))

    def attend_late(stats):
        wide = 16 * len(late_rows)
        index = lax.broadcasted_iota(jnp.int32, (QPK, wide), 1)
        device = jnp.zeros((QPK, wide), jnp.int32)
        n = 0
        for c in LATE:
            for offset, dx in CHUNKS[c]:
                device = jnp.where(index // 16 == n, x_parts[dx] + pair_parts[offset], device)
                n += 1
        device = device + (index % 16) // PAGE
        position = device * (SPLIT * PAGE) + part * PAGE + index % PAGE
        for eight in range(CAP // 8):
            slots = [eight * 8 + k for k in range(8)]
            rows = [
                scale_rows(jnp.concatenate([scales[slot, at, :] for at in late_rows], axis=0))
                for slot in slots
            ]
            tokens = [
                jnp.concatenate([cache[slot, at, :] for at in late_rows], axis=0)
                for slot in slots
            ]
            numerator, highest, weight_sum = attend(
                [query_ref[RES + slot].astype(jnp.bfloat16) for slot in slots],
                [each[:, :HD] for each in tokens],
                [each[:, HD:] for each in tokens],
                [(each[0:1], each[PAGE : PAGE + 1]) for each in rows],
                [position < slot_length[slot] for slot in slots],
            )
            tops = [jnp.maximum(early_highest[slots[k]], highest[k]) for k in range(8)]
            early_factors = [jnp.exp(early_highest[slots[k]] - tops[k]) for k in range(8)]
            factors = [jnp.exp(highest[k] - tops[k]) for k in range(8)]
            numerators = [
                early_numerator[slots[k]] * early_factors[k] + numerator[k] * factors[k]
                for k in range(8)
            ]
            for k in range(8):
                total = early_sum[slots[k]] * early_factors[k] + weight_sum[k] * factors[k]
                stats = keep(RES + slots[k], tops[k], total, stats)
            put(1 + eight * 2, numerators[:4])
            put(2 + eight * 2, numerators[4:])
        return stats

    store(0)
    forward(2)
    store(1)
    forward(3)
    attend_early()
    forward(4)
    store(2)
    store(3)
    store(4)
    stats = attend_late(stats)
    for s in range(SPLIT):
        stat_send[s, :SHARE] = stats[0][s * SHARE : (s + 1) * SHARE]
        stat_send[s, SHARE:] = stats[1][s * SHARE : (s + 1) * SHARE]

    for k in range(1, SPLIT):
        s = lax.rem(part + k, SPLIT)
        to = (group, head * SPLIT + s)
        pltpu.make_async_remote_copy(
            src_ref=stat_send.at[s],
            dst_ref=stat_got.at[part],
            send_sem=stat_sem.at[0],
            recv_sem=stat_sem.at[1],
            device_id=to,
            device_id_type=MESH,
        ).start()
    send_parts(pl.ds(RES * SHARE, CAP * SHARE))
    stat_got[part] = stat_send[part]
    part_got[part] = part_send[part]

    @pl.loop(0, CAP // 4)
    def _(four):
        slots = [four * 4 + k for k in range(4)]
        rows = [scale_rows(scales[slot]).astype(jnp.bfloat16) for slot in slots]
        for k, slot in enumerate(slots):
            scale_rows_ref[slot, 0:1, :] = rows[k][0:1]
            scale_rows_ref[slot, 1:2, :] = rows[k][PAGE : PAGE + 1]

    scale_copy = pltpu.make_async_copy(scale_rows_ref, scale_out_ref, local_sem.at[2])
    scale_copy.start()

    three_stats = stat_got.at[pl.ds(0, SPLIT - 1)]
    three_parts = part_got.at[pl.ds(0, SPLIT - 1)]
    pltpu.make_async_copy(three_stats, three_stats, stat_sem.at[1]).wait()
    highest = [stat_got[s, :SHARE] for s in range(SPLIT)]
    top = functools.reduce(jnp.maximum, highest)
    factors = [jnp.exp(each - top) for each in highest]
    total = functools.reduce(jnp.add, [stat_got[s, SHARE:] * factors[s] for s in range(SPLIT)])
    total = jnp.maximum(total, 1.0)
    factors = [each / total for each in factors]
    pltpu.make_async_copy(three_parts, three_parts, part_sem.at[1]).wait()
    parts = [part_got[s].astype(jnp.float32) for s in range(SPLIT)]
    for r in range(ROWS):
        merged = functools.reduce(
            jnp.add,
            [
                parts[s][r * SHARE : (r + 1) * SHARE] * factors[s][:, r : r + 1]
                for s in range(SPLIT)
            ],
        )
        for q in range(SHARE):
            merged_ref[r : r + 1, q * HD : (q + 1) * HD] = merged[q : q + 1]
    attended_ref[...] = merged_ref[...].astype(jnp.bfloat16)
    attended_copy = pltpu.make_async_copy(attended_ref, attended_out_ref, local_sem.at[3])
    attended_copy.start()

    sent = send1.at[pl.ds(0, DEVS - 1)]
    pltpu.make_async_copy(sent, sent, send1_sem).wait()
    for c in range(len(CHUNKS)):
        sent = send2[c].at[pl.ds(0, GROUPS - 1)]
        pltpu.make_async_copy(sent, sent, send2_sem.at[c]).wait()
    sent = meta_send.at[pl.ds(0, GROUPS - 1)]
    pltpu.make_async_copy(sent, sent, meta_sem.at[0]).wait()
    sent = stat_send.at[pl.ds(0, SPLIT - 1)]
    pltpu.make_async_copy(sent, sent, stat_sem.at[0]).wait()
    sent = part_send.at[pl.ds(0, SPLIT - 1)]
    pltpu.make_async_copy(sent, sent, part_sem.at[0]).wait()
    pltpu.make_async_copy(cache, cache_out_ref, cache_sem).wait()
    scale_copy.wait()
    attended_copy.wait()


def copy_kernel(
    attended_in,
    cache_in,
    scale_in,
    attended_out,
    cache_out,
    scale_out,
    attended_held,
    cache_held,
    scale_held,
    in_sem,
    out_sem,
):
    pieces = [
        (cache_in.at[at], cache_held.at[at], cache_out.at[at])
        for at in (pl.ds(i * 2, 2) for i in range(CAP // 2))
    ]
    pieces.append((scale_in, scale_held, scale_out))
    pieces.append((attended_in, attended_held, attended_out))
    loads = [pltpu.make_async_copy(p[0], p[1], in_sem.at[i]) for i, p in enumerate(pieces)]
    stores = [pltpu.make_async_copy(p[1], p[2], out_sem.at[i]) for i, p in enumerate(pieces)]
    for load in loads:
        load.start()
    for load, store in zip(loads, stores):
        load.wait()
        store.start()
    for store in stores:
        store.wait()


def body(
    prefill_pool,
    page_table,
    req_lengths,
    dest_group,
    resident_kv,
    resident_scale,
    res_lengths,
    queries,
):
    hbm = pl.BlockSpec(memory_space=pltpu.HBM)
    bf16 = jnp.bfloat16
    out_shape = (
        jax.ShapeDtypeStruct((ROWS, SHARE * HD), bf16),
        jax.ShapeDtypeStruct((CAP, TOKENS, 2 * HD), bf16),
        jax.ShapeDtypeStruct((CAP, 2, TOKENS), bf16),
    )
    results = pl.pallas_call(
        kernel,
        out_shape=out_shape,
        in_specs=[hbm] * 8,
        out_specs=(hbm,) * 3,
        scratch_shapes=[
            pltpu.SMEM((1, 1, REQ * SPLIT), jnp.int32),
            pltpu.SMEM((REQ,), jnp.int32),
            pltpu.SMEM((REQ,), jnp.int32),
            pltpu.SMEM((RES,), jnp.int32),
            pltpu.VMEM((REQ * SPLIT, PAGE, 2 * KVH * HD), bf16),
            pltpu.VMEM((ROWS, QPK * HD), bf16),
            pltpu.VMEM((RES, RES_TOKENS, 2 * HD), bf16),
            pltpu.VMEM((RES, 2, RES_TOKENS), bf16),
            pltpu.VMEM((ROWS, QPK, HD), jnp.float32),
            pltpu.VMEM((DEVS, REQ, 2 * PAGE, HD), bf16),
            *[pltpu.VMEM((n, REQ, 2 * PAGE, HD), bf16) for n in COUNTS],
            *[pltpu.VMEM((GROUPS, n, 2 * PAGE, HD), bf16) for n in COUNTS],
            *[pltpu.VMEM((GROUPS, n, 2 * PAGE, HD), bf16) for n in COUNTS],
            pltpu.VMEM((GROUPS, 1, 128), jnp.int32),
            pltpu.VMEM((GROUPS, 1, 128), jnp.int32),
            pltpu.SMEM((GROUPS, 1, 128), jnp.int32),
            pltpu.SMEM((GROUPS,), jnp.int32),
            pltpu.SMEM((CAP,), jnp.int32),
            pltpu.SMEM((CAP,), jnp.int32),
            pltpu.VMEM((CAP, TOKENS, 2 * HD), bf16),
            pltpu.VMEM((CAP, TOKENS, 128), bf16),
            *[pltpu.VMEM((CAP, QPK, HD), jnp.float32)] * 3,
            pltpu.VMEM((CAP, 2, TOKENS), bf16),
            pltpu.VMEM((ROWS, SHARE * HD), jnp.float32),
            pltpu.VMEM((ROWS, SHARE * HD), bf16),
            pltpu.VMEM((SPLIT, ROWS * SHARE, HD), jnp.float32),
            pltpu.VMEM((SPLIT, ROWS * SHARE, HD), jnp.float32),
            pltpu.VMEM((SPLIT, 2 * SHARE, 128), jnp.float32),
            pltpu.VMEM((SPLIT, 2 * SHARE, 128), jnp.float32),
            pltpu.SemaphoreType.DMA,
            pltpu.SemaphoreType.DMA((len(CHUNKS),)),
            pltpu.SemaphoreType.DMA((len(CHUNKS),)),
            pltpu.SemaphoreType.DMA((len(CHUNKS),)),
            pltpu.SemaphoreType.DMA((2,)),
            pltpu.SemaphoreType.DMA((2,)),
            pltpu.SemaphoreType.DMA((2,)),
            pltpu.SemaphoreType.DMA((4,)),
            pltpu.SemaphoreType.DMA,
            pltpu.SemaphoreType.DMA((8,)),
            pltpu.SemaphoreType.REGULAR((3,)),
        ],
        compiler_params=pltpu.CompilerParams(
            collective_id=0, has_side_effects=True, vmem_limit_bytes=62 * 2**20
        ),
        name="migrate_and_attend",
    )(
        page_table,
        dest_group,
        req_lengths,
        res_lengths,
        prefill_pool,
        queries,
        resident_kv,
        jnp.swapaxes(resident_scale, 1, 2),
    )
    attended, migrated_cache, migrated_scale = pl.pallas_call(
        copy_kernel,
        out_shape=out_shape,
        in_specs=[hbm] * 3,
        out_specs=(hbm,) * 3,
        scratch_shapes=[
            *[pltpu.VMEM(each.shape, each.dtype) for each in out_shape],
            pltpu.SemaphoreType.DMA((CAP // 2 + 2,)),
            pltpu.SemaphoreType.DMA((CAP // 2 + 2,)),
        ],
        compiler_params=pltpu.CompilerParams(vmem_limit_bytes=62 * 2**20),
        name="copy_results",
    )(*results)
    return attended, migrated_cache, jnp.swapaxes(migrated_scale, 1, 2)


def solution(mesh):
    return jax.shard_map(
        body,
        mesh=mesh,
        in_specs=(
            P("group", "dev", None),
            P("group", "dev", None),
            P("group"),
            P("group"),
            P("group", "dev", None),
            P("group", "dev", None),
            P("group"),
            P("group", None),
        ),
        out_specs=(P("group", "dev"), P("group", "dev", None), P("group", "dev", None)),
        check_vma=False,
    )
```

```python
import functools
import math

import jax
import jax.numpy as jnp
from jax import lax
from jax.experimental import pallas as pl
from jax.experimental.pallas import tpu as pltpu
from jax.sharding import PartitionSpec as P

KVH = 8
HD = 128
QPK = 16
PAGE = 8
GROUPS = 16
DEVS = 32
SPLIT = 4
REQ = 8
RES = 4
CAP = 16
ROWS = RES + CAP
TOKENS = DEVS * PAGE
RES_TOKENS = 512
SHARE = QPK // SPLIT

TINY = 1e-06
LEVEL = 448.0
NONE = -1e30
MESH = pl.DeviceIdType.MESH

CHUNKS = (
    ((0, 0), (0, 1), (1, 0), (1, 1), (7, 0), (7, 1)),
    ((2, 0), (2, 1), (6, 0), (6, 1)),
    ((3, 0), (3, 1), (5, 0), (5, 1)),
    ((4, 0),),
    ((4, 1),),
)
COUNTS = tuple(2 * len(chunk) for chunk in CHUNKS)
LATE = (2, 3, 4)


def attend(queries, keys, values, scales, usable):
    count = len(queries)
    scores = [
        lax.dot_general(
            queries[i], keys[i], (((1,), (1,)), ((), ())), preferred_element_type=jnp.float32
        )
        for i in range(count)
    ]
    scores = [
        jnp.where(usable[i], scores[i] * (scales[i][0] * (1.0 / math.sqrt(HD))), NONE)
        for i in range(count)
    ]
    highest = [jnp.max(each, axis=1, keepdims=True) for each in scores]
    raised = [
        jnp.where(usable[i], jnp.exp(scores[i] - highest[i]), 0.0) for i in range(count)
    ]
    weight_sum = [jnp.sum(each, axis=1, keepdims=True) for each in raised]
    numerator = [
        jnp.dot(
            (raised[i] * scales[i][1]).astype(jnp.bfloat16),
            values[i],
            preferred_element_type=jnp.float32,
        )
        for i in range(count)
    ]
    return numerator, highest, weight_sum


def kernel(
    table_hbm,
    dest_hbm,
    length_hbm,
    res_length_hbm,
    pool_hbm,
    query_hbm,
    res_kv_hbm,
    res_scale_hbm,
    part_got,
    stat_got,
    cache_out_ref,
    scale_out_ref,
    table_ref,
    dest_ref,
    length_ref,
    res_length_ref,
    pool_ref,
    query_in,
    res_kv_ref,
    res_scale_ref,
    query_ref,
    send1,
    got1_0,
    got1_1,
    got1_2,
    got1_3,
    got1_4,
    send2_0,
    send2_1,
    send2_2,
    send2_3,
    send2_4,
    got2_0,
    got2_1,
    got2_2,
    got2_3,
    got2_4,
    meta_send,
    meta_got,
    meta_smem,
    picked,
    slot_source,
    slot_length,
    cache,
    scales,
    early_numerator,
    early_highest,
    early_sum,
    scale_rows_ref,
    part_send,
    stat_send,
    send1_sem,
    got1_sem,
    send2_sem,
    got2_sem,
    meta_sem,
    part_sem,
    stat_sem,
    local_sem,
    cache_sem,
    in_sem,
    ready_sem,
):
    got1 = (got1_0, got1_1, got1_2, got1_3, got1_4)
    send2 = (send2_0, send2_1, send2_2, send2_3, send2_4)
    got2 = (got2_0, got2_1, got2_2, got2_3, got2_4)
    group = lax.axis_index("group")
    dev = lax.axis_index("dev")
    x_hi = dev // 16
    pair = (dev % 16) // 2
    parity = dev % 2
    head = dev // SPLIT
    part = dev % SPLIT

    x_parts = (x_hi * 16, (1 - x_hi) * 16)
    pair_parts = [lax.rem(pair + k, 8) * 2 for k in range(8)]
    parities = (parity, 1 - parity)

    def peer_dev(offset, dx, dp):
        return x_parts[dx] + pair_parts[offset] + parities[dp]

    def request_for(target):
        picked = jnp.int32(0)
        for j in range(REQ):
            picked = jnp.where(dest_ref[j] == target, j, picked)
        return picked

    def length_for(target):
        picked = jnp.int32(0)
        for j in range(REQ):
            picked = jnp.where(dest_ref[j] == target, length_ref[j], picked)
        return picked

    loads = [
        pltpu.make_async_copy(source, target, in_sem.at[i])
        for i, (source, target) in enumerate(
            (
                (pool_hbm, pool_ref),
                (table_hbm, table_ref),
                (dest_hbm, dest_ref),
                (length_hbm, length_ref),
                (res_length_hbm, res_length_ref),
                (
                    query_hbm.at[:, pl.ds(pl.multiple_of(head * (QPK * HD), 128), QPK * HD)],
                    query_in,
                ),
                (res_kv_hbm, res_kv_ref),
                (res_scale_hbm, res_scale_ref),
            )
        )
    ]
    for load in loads[:5]:
        load.start()

    barrier = pltpu.get_barrier_semaphore()
    near = [
        (offset, dx, dp)
        for offset, dx in CHUNKS[0]
        for dp in range(2)
        if (offset, dx, dp) != (0, 0, 0)
    ]
    for peer in near:
        pl.semaphore_signal(
            barrier, inc=1, device_id=(group, peer_dev(*peer)), device_id_type=MESH
        )

    @pl.loop(1, GROUPS)
    def _(k):
        pl.semaphore_signal(
            barrier, inc=1, device_id=(lax.rem(group + k, GROUPS), dev), device_id_type=MESH
        )

    for load in loads[:5]:
        load.wait()
    for load in loads[5:]:
        load.start()

    @pl.loop(0, REQ)
    def _(j):
        for s in range(SPLIT):
            page = pool_ref[table_ref[0, 0, j * SPLIT + s]].astype(jnp.float32)
            for h in range(KVH):
                block = jnp.concatenate(
                    [
                        page[:, h * HD : (h + 1) * HD],
                        page[:, (KVH + h) * HD : (KVH + h + 1) * HD],
                    ],
                    axis=0,
                )
                send1[h * SPLIT + s, j] = block.astype(jnp.bfloat16)

    pl.semaphore_wait(barrier, len(near) + GROUPS - 1)

    def start(c):
        for dp in range(2):
            for offset, dx in CHUNKS[c]:
                if (offset, dx, dp) == (0, 0, 0):
                    continue
                to = peer_dev(offset, dx, dp)
                place = CHUNKS[c].index(((8 - offset) % 8, dx)) * 2 + parity
                pltpu.make_async_remote_copy(
                    src_ref=send1.at[to],
                    dst_ref=got1[c].at[place],
                    send_sem=send1_sem,
                    recv_sem=got1_sem.at[c],
                    device_id=(group, to),
                    device_id_type=MESH,
                ).start()

    def round_over(i):
        for offset in (1, 7):
            pl.semaphore_signal(
                ready_sem.at[i],
                inc=1,
                device_id=(group, peer_dev(offset, 0, 0)),
                device_id_type=MESH,
            )

    def await_round(i):
        pl.semaphore_wait(ready_sem.at[i], 2)

    round_over(0)
    start(0)
    await_round(0)
    round_over(1)
    start(1)
    await_round(1)
    round_over(2)
    start(2)
    await_round(2)
    start(3)
    start(4)

    @pl.loop(0, GROUPS)
    def _(g):
        meta_send[g] = jnp.full((1, 128), length_for(g), jnp.int32)
        picked[g] = request_for(g)

    @pl.loop(1, GROUPS)
    def _(k):
        to = lax.rem(group + k, GROUPS)
        pltpu.make_async_remote_copy(
            src_ref=meta_send.at[to],
            dst_ref=meta_got.at[group],
            send_sem=meta_sem.at[0],
            recv_sem=meta_sem.at[1],
            device_id=(to, dev),
            device_id_type=MESH,
        ).start()

    got1[0][parity] = send1[dev]
    meta_got[group] = meta_send[group]

    for load in loads[5:]:
        load.wait()
    heads = query_in[...].astype(jnp.float32)
    for q in range(QPK):
        query_ref[:, q, :] = heads[:, q * HD : (q + 1) * HD]
    lane16 = lax.broadcasted_iota(jnp.int32, (QPK, 128), 1)
    stat_highest = jnp.zeros((QPK, 128), jnp.float32)
    stat_sum = jnp.zeros((QPK, 128), jnp.float32)

    def keep(row, highest, weight_sum, stats):
        here = lane16 == row
        return jnp.where(here, highest, stats[0]), jnp.where(here, weight_sum, stats[1])

    def put(four, numerators):
        for s in range(SPLIT):
            share = [each[s * SHARE : (s + 1) * SHARE] for each in numerators]
            part_send[s, four * 16 : (four + 1) * 16] = jnp.concatenate(share, axis=0).astype(
                part_send.dtype
            )

    stats = (stat_highest, stat_sum)
    res_position = part * RES_TOKENS + lax.broadcasted_iota(jnp.int32, (QPK, RES_TOKENS), 1)
    row_scales = [res_scale_ref[r].astype(jnp.float32) for r in range(RES)]
    numerators, highest, weight_sum = attend(
        [query_ref[r].astype(jnp.bfloat16) for r in range(RES)],
        [res_kv_ref[r, :, :HD] for r in range(RES)],
        [res_kv_ref[r, :, HD:] for r in range(RES)],
        [(each[0:1], each[1:2]) for each in row_scales],
        [res_position < res_length_ref[r] for r in range(RES)],
    )
    for r in range(RES):
        stats = keep(r, highest[r], weight_sum[r], stats)
    put(0, numerators)

    def send_parts(rows):
        for k in range(1, SPLIT):
            s = lax.rem(part + k, SPLIT)
            pltpu.make_async_remote_copy(
                src_ref=part_send.at[s, rows],
                dst_ref=part_got.at[part, rows],
                send_sem=part_sem.at[0],
                recv_sem=part_sem.at[1],
                device_id=(group, head * SPLIT + s),
                device_id_type=MESH,
            ).start()

    send_parts(pl.ds(0, RES * SHARE))

    def rows_of(c):
        return [
            pl.ds(pl.multiple_of((x_parts[dx] + pair_parts[offset]) * PAGE, 16), 16)
            for offset, dx in CHUNKS[c]
        ]

    late_rows = [at for c in LATE for at in rows_of(c)]

    @pl.loop(0, CAP)
    def _(slot):
        for at in late_rows:
            cache[slot, at, :] = jnp.zeros((16, 2 * HD), jnp.bfloat16)
            scales[slot, at, :] = jnp.zeros((16, 128), jnp.bfloat16)

    def forward(c):
        count = COUNTS[c]
        taken = count - 1 if c == 0 else count
        arrived = got1[c].at[pl.ds(0, taken)]
        pltpu.make_async_copy(arrived, arrived, got1_sem.at[c]).wait()
        got2[c][group] = got1[c][:, picked[group]]

        @pl.loop(0, 3)
        def _(third):
            targets = [lax.rem(group + third * 5 + k, GROUPS) for k in range(1, 6)]
            for to in targets:
                send2[c][to] = got1[c][:, picked[to]]
            for to in targets:
                pltpu.make_async_remote_copy(
                    src_ref=send2[c].at[to],
                    dst_ref=got2[c].at[group],
                    send_sem=send2_sem.at[c],
                    recv_sem=got2_sem.at[c],
                    device_id=(to, dev),
                    device_id_type=MESH,
                ).start()

    lane_rows = lax.broadcasted_iota(jnp.int32, (16, 128), 1)

    def store(c):
        count = COUNTS[c]
        others = got2[c].at[pl.ds(0, GROUPS - 1)]
        pltpu.make_async_copy(others, others, got2_sem.at[c]).wait()

        places = rows_of(c)

        @pl.loop(0, CAP // 2)
        def _(two):
            for k in range(2):
                slot = two * 2 + k
                present = slot_length[slot] > 0
                block = got2[c][slot_source[slot]].astype(jnp.float32)
                block = jnp.where(present, block, 0.0)
                peak = jnp.max(jnp.abs(block), axis=2, keepdims=True)
                scale = ((peak + TINY) / LEVEL).astype(jnp.bfloat16).astype(jnp.float32)
                stored = block * (1.0 / scale)
                scale = jnp.broadcast_to(jnp.where(present, scale, 0.0), block.shape)
                for i, at in enumerate(places):
                    n = i * 2
                    for kind in range(2):
                        rows = slice(kind * PAGE, (kind + 1) * PAGE)
                        both = jnp.concatenate([stored[n, rows], stored[n + 1, rows]], axis=0)
                        cache[slot, at, kind * HD : (kind + 1) * HD] = both.astype(jnp.bfloat16)
                    key_scale = jnp.concatenate([scale[n, :PAGE], scale[n + 1, :PAGE]], axis=0)
                    value_scale = jnp.concatenate([scale[n, PAGE:], scale[n + 1, PAGE:]], axis=0)
                    scales[slot, at] = jnp.where(lane_rows == 0, key_scale, value_scale).astype(
                        jnp.bfloat16
                    )

        for at in places:
            pltpu.make_async_copy(
                cache.at[:, at, :], cache_out_ref.at[:, at, :], cache_sem
            ).start()

    forward(0)
    forward(1)

    metas = meta_got.at[pl.ds(0, GROUPS - 1)]
    pltpu.make_async_copy(metas, metas, meta_sem.at[1]).wait()
    pltpu.make_async_copy(meta_got, meta_smem, local_sem.at[0]).start()
    pltpu.make_async_copy(meta_got, meta_smem, local_sem.at[0]).wait()

    @pl.loop(0, CAP)
    def _(slot):
        source = jnp.int32(0)
        length = jnp.int32(0)
        rank = jnp.int32(0)
        for g in range(GROUPS):
            this_length = meta_smem[g, 0, 0]
            here = jnp.logical_and(this_length > 0, rank == slot)
            source = jnp.where(here, g, source)
            length = jnp.where(here, this_length, length)
            rank = rank + jnp.where(this_length > 0, 1, 0)
        slot_source[slot] = source
        slot_length[slot] = length

    row16 = lax.broadcasted_iota(jnp.int32, (QPK, 128), 0)
    pick = jnp.where(lane16 == row16 // PAGE, 1.0, 0.0).astype(jnp.bfloat16)

    def scale_rows(block):
        return lax.dot_general(
            pick, block, (((1,), (1,)), ((), ())), preferred_element_type=jnp.float32
        )

    def attend_early():
        index = lax.broadcasted_iota(jnp.int32, (QPK, TOKENS), 1)
        device = index // PAGE
        position = device * (SPLIT * PAGE) + part * PAGE + index % PAGE
        its_pair = (device % 16) // 2
        early = its_pair >= 0
        for c in LATE:
            for offset, _ in CHUNKS[c]:
                early = jnp.logical_and(early, its_pair * 2 != pair_parts[offset])

        @pl.loop(0, CAP // 4)
        def _(four):
            slots = [four * 4 + k for k in range(4)]
            rows = [scale_rows(scales[slot]) for slot in slots]
            numerator, highest, weight_sum = attend(
                [query_ref[RES + slot].astype(jnp.bfloat16) for slot in slots],
                [cache[slot, :, :HD] for slot in slots],
                [cache[slot, :, HD:] for slot in slots],
                [(each[0:1], each[PAGE : PAGE + 1]) for each in rows],
                [jnp.logical_and(early, position < slot_length[slot]) for slot in slots],
            )
            for k, slot in enumerate(slots):
                early_numerator[slot] = numerator[k]
                early_highest[slot] = jnp.broadcast_to(highest[k], (QPK, 128))
                early_sum[slot] = jnp.broadcast_to(weight_sum[k], (QPK, 128))

    def attend_late(stats):
        wide = 16 * len(late_rows)
        index = lax.broadcasted_iota(jnp.int32, (QPK, wide), 1)
        device = jnp.zeros((QPK, wide), jnp.int32)
        n = 0
        for c in LATE:
            for offset, dx in CHUNKS[c]:
                device = jnp.where(index // 16 == n, x_parts[dx] + pair_parts[offset], device)
                n += 1
        device = device + (index % 16) // PAGE
        position = device * (SPLIT * PAGE) + part * PAGE + index % PAGE
        for eight in range(CAP // 8):
            slots = [eight * 8 + k for k in range(8)]
            rows = [
                scale_rows(jnp.concatenate([scales[slot, at, :] for at in late_rows], axis=0))
                for slot in slots
            ]
            tokens = [
                jnp.concatenate([cache[slot, at, :] for at in late_rows], axis=0)
                for slot in slots
            ]
            numerator, highest, weight_sum = attend(
                [query_ref[RES + slot].astype(jnp.bfloat16) for slot in slots],
                [each[:, :HD] for each in tokens],
                [each[:, HD:] for each in tokens],
                [(each[0:1], each[PAGE : PAGE + 1]) for each in rows],
                [position < slot_length[slot] for slot in slots],
            )
            tops = [jnp.maximum(early_highest[slots[k]], highest[k]) for k in range(8)]
            early_factors = [jnp.exp(early_highest[slots[k]] - tops[k]) for k in range(8)]
            factors = [jnp.exp(highest[k] - tops[k]) for k in range(8)]
            numerators = [
                early_numerator[slots[k]] * early_factors[k] + numerator[k] * factors[k]
                for k in range(8)
            ]
            for k in range(8):
                total = early_sum[slots[k]] * early_factors[k] + weight_sum[k] * factors[k]
                stats = keep(RES + slots[k], tops[k], total, stats)
            put(1 + eight * 2, numerators[:4])
            put(2 + eight * 2, numerators[4:])
        return stats

    store(0)
    forward(2)
    store(1)
    forward(3)
    attend_early()
    forward(4)
    store(2)
    store(3)
    store(4)
    stats = attend_late(stats)
    for s in range(SPLIT):
        stat_send[s, :SHARE] = stats[0][s * SHARE : (s + 1) * SHARE]
        stat_send[s, SHARE:] = stats[1][s * SHARE : (s + 1) * SHARE]

    for k in range(1, SPLIT):
        s = lax.rem(part + k, SPLIT)
        to = (group, head * SPLIT + s)
        pltpu.make_async_remote_copy(
            src_ref=stat_send.at[s],
            dst_ref=stat_got.at[part],
            send_sem=stat_sem.at[0],
            recv_sem=stat_sem.at[1],
            device_id=to,
            device_id_type=MESH,
        ).start()
    send_parts(pl.ds(RES * SHARE, CAP * SHARE))
    own_copies = [
        pltpu.make_async_copy(stat_send.at[part], stat_got.at[part], local_sem.at[1]),
        pltpu.make_async_copy(part_send.at[part], part_got.at[part], local_sem.at[3]),
    ]
    for own_copy in own_copies:
        own_copy.start()

    @pl.loop(0, CAP // 4)
    def _(four):
        slots = [four * 4 + k for k in range(4)]
        rows = [scale_rows(scales[slot]).astype(jnp.bfloat16) for slot in slots]
        for k, slot in enumerate(slots):
            scale_rows_ref[slot, 0:1, :] = rows[k][0:1]
            scale_rows_ref[slot, 1:2, :] = rows[k][PAGE : PAGE + 1]

    scale_copy = pltpu.make_async_copy(scale_rows_ref, scale_out_ref, local_sem.at[2])
    scale_copy.start()

    three_stats = stat_got.at[pl.ds(0, SPLIT - 1)]
    three_parts = part_got.at[pl.ds(0, SPLIT - 1)]
    pltpu.make_async_copy(three_stats, three_stats, stat_sem.at[1]).wait()
    pltpu.make_async_copy(three_parts, three_parts, part_sem.at[1]).wait()

    sent = send1.at[pl.ds(0, DEVS - 1)]
    pltpu.make_async_copy(sent, sent, send1_sem).wait()
    for c in range(len(CHUNKS)):
        sent = send2[c].at[pl.ds(0, GROUPS - 1)]
        pltpu.make_async_copy(sent, sent, send2_sem.at[c]).wait()
    sent = meta_send.at[pl.ds(0, GROUPS - 1)]
    pltpu.make_async_copy(sent, sent, meta_sem.at[0]).wait()
    sent = stat_send.at[pl.ds(0, SPLIT - 1)]
    pltpu.make_async_copy(sent, sent, stat_sem.at[0]).wait()
    sent = part_send.at[pl.ds(0, SPLIT - 1)]
    pltpu.make_async_copy(sent, sent, part_sem.at[0]).wait()
    pltpu.make_async_copy(cache, cache_out_ref, cache_sem).wait()
    scale_copy.wait()
    for own_copy in own_copies:
        own_copy.wait()


def finish_kernel(
    part_in,
    stat_in,
    cache_in,
    scale_in,
    attended_out,
    cache_out,
    scale_out,
    part_got,
    stat_got,
    attended_ref,
    cache_held,
    scale_held,
    merged_ref,
    in_sem,
    out_sem,
    part_sem,
):
    pieces = [
        (cache_in.at[at], cache_held.at[at], cache_out.at[at])
        for at in (pl.ds(i * 2, 2) for i in range(CAP // 2))
    ]
    pieces.append((scale_in, scale_held, scale_out))
    loads = [pltpu.make_async_copy(p[0], p[1], in_sem.at[i]) for i, p in enumerate(pieces)]
    stores = [pltpu.make_async_copy(p[1], p[2], out_sem.at[i]) for i, p in enumerate(pieces)]
    stat_load = pltpu.make_async_copy(stat_in, stat_got, part_sem.at[0])
    part_load = pltpu.make_async_copy(part_in, part_got, part_sem.at[1])
    stat_load.start()
    part_load.start()
    for load in loads:
        load.start()
    for load, store in zip(loads, stores):
        load.wait()
        store.start()
    stat_load.wait()
    part_load.wait()
    highest = [stat_got[s, :SHARE] for s in range(SPLIT)]
    top = functools.reduce(jnp.maximum, highest)
    factors = [jnp.exp(each - top) for each in highest]
    total = functools.reduce(jnp.add, [stat_got[s, SHARE:] * factors[s] for s in range(SPLIT)])
    total = jnp.maximum(total, 1.0)
    factors = [each / total for each in factors]
    parts = [part_got[s] for s in range(SPLIT)]
    for r in range(ROWS):
        merged = functools.reduce(
            jnp.add,
            [
                parts[s][r * SHARE : (r + 1) * SHARE] * factors[s][:, r : r + 1]
                for s in range(SPLIT)
            ],
        )
        for q in range(SHARE):
            merged_ref[r : r + 1, q * HD : (q + 1) * HD] = merged[q : q + 1]
    attended_ref[...] = merged_ref[...].astype(jnp.bfloat16)
    attended_store = pltpu.make_async_copy(attended_ref, attended_out, part_sem.at[2])
    attended_store.start()
    for store in stores:
        store.wait()
    attended_store.wait()


def body(
    prefill_pool,
    page_table,
    req_lengths,
    dest_group,
    resident_kv,
    resident_scale,
    res_lengths,
    queries,
):
    hbm = pl.BlockSpec(memory_space=pltpu.HBM)
    bf16 = jnp.bfloat16
    cache_shape = jax.ShapeDtypeStruct((CAP, TOKENS, 2 * HD), bf16)
    scale_shape = jax.ShapeDtypeStruct((CAP, 2, TOKENS), bf16)
    part_shape = jax.ShapeDtypeStruct((SPLIT, ROWS * SHARE, HD), jnp.float32)
    stat_shape = jax.ShapeDtypeStruct((SPLIT, 2 * SHARE, 128), jnp.float32)
    attended_shape = jax.ShapeDtypeStruct((ROWS, SHARE * HD), bf16)
    results = pl.pallas_call(
        kernel,
        out_shape=(part_shape, stat_shape, cache_shape, scale_shape),
        in_specs=[hbm] * 8,
        out_specs=(hbm,) * 4,
        scratch_shapes=[
            pltpu.SMEM((1, 1, REQ * SPLIT), jnp.int32),
            pltpu.SMEM((REQ,), jnp.int32),
            pltpu.SMEM((REQ,), jnp.int32),
            pltpu.SMEM((RES,), jnp.int32),
            pltpu.VMEM((REQ * SPLIT, PAGE, 2 * KVH * HD), bf16),
            pltpu.VMEM((ROWS, QPK * HD), bf16),
            pltpu.VMEM((RES, RES_TOKENS, 2 * HD), bf16),
            pltpu.VMEM((RES, 2, RES_TOKENS), bf16),
            pltpu.VMEM((ROWS, QPK, HD), jnp.float32),
            pltpu.VMEM((DEVS, REQ, 2 * PAGE, HD), bf16),
            *[pltpu.VMEM((n, REQ, 2 * PAGE, HD), bf16) for n in COUNTS],
            *[pltpu.VMEM((GROUPS, n, 2 * PAGE, HD), bf16) for n in COUNTS],
            *[pltpu.VMEM((GROUPS, n, 2 * PAGE, HD), bf16) for n in COUNTS],
            pltpu.VMEM((GROUPS, 1, 128), jnp.int32),
            pltpu.VMEM((GROUPS, 1, 128), jnp.int32),
            pltpu.SMEM((GROUPS, 1, 128), jnp.int32),
            pltpu.SMEM((GROUPS,), jnp.int32),
            pltpu.SMEM((CAP,), jnp.int32),
            pltpu.SMEM((CAP,), jnp.int32),
            pltpu.VMEM((CAP, TOKENS, 2 * HD), bf16),
            pltpu.VMEM((CAP, TOKENS, 128), bf16),
            *[pltpu.VMEM((CAP, QPK, HD), jnp.float32)] * 3,
            pltpu.VMEM((CAP, 2, TOKENS), bf16),
            pltpu.VMEM((SPLIT, ROWS * SHARE, HD), jnp.float32),
            pltpu.VMEM((SPLIT, 2 * SHARE, 128), jnp.float32),
            pltpu.SemaphoreType.DMA,
            pltpu.SemaphoreType.DMA((len(CHUNKS),)),
            pltpu.SemaphoreType.DMA((len(CHUNKS),)),
            pltpu.SemaphoreType.DMA((len(CHUNKS),)),
            pltpu.SemaphoreType.DMA((2,)),
            pltpu.SemaphoreType.DMA((2,)),
            pltpu.SemaphoreType.DMA((2,)),
            pltpu.SemaphoreType.DMA((4,)),
            pltpu.SemaphoreType.DMA,
            pltpu.SemaphoreType.DMA((8,)),
            pltpu.SemaphoreType.REGULAR((3,)),
        ],
        compiler_params=pltpu.CompilerParams(
            collective_id=0, has_side_effects=True, vmem_limit_bytes=62 * 2**20
        ),
        name="migrate_and_attend",
    )(
        page_table,
        dest_group,
        req_lengths,
        res_lengths,
        prefill_pool,
        queries,
        resident_kv,
        jnp.swapaxes(resident_scale, 1, 2),
    )
    held = (part_shape, stat_shape, attended_shape, cache_shape, scale_shape)
    attended, migrated_cache, migrated_scale = pl.pallas_call(
        finish_kernel,
        out_shape=(attended_shape, cache_shape, scale_shape),
        in_specs=[hbm] * 4,
        out_specs=(hbm,) * 3,
        scratch_shapes=[
            *[pltpu.VMEM(each.shape, each.dtype) for each in held],
            pltpu.VMEM(attended_shape.shape, jnp.float32),
            pltpu.SemaphoreType.DMA((CAP // 2 + 1,)),
            pltpu.SemaphoreType.DMA((CAP // 2 + 1,)),
            pltpu.SemaphoreType.DMA((3,)),
        ],
        compiler_params=pltpu.CompilerParams(vmem_limit_bytes=62 * 2**20),
        name="merge_and_copy",
    )(*results)
    return attended, migrated_cache, jnp.swapaxes(migrated_scale, 1, 2)


def solution(mesh):
    return jax.shard_map(
        body,
        mesh=mesh,
        in_specs=(
            P("group", "dev", None),
            P("group", "dev", None),
            P("group"),
            P("group"),
            P("group", "dev", None),
            P("group", "dev", None),
            P("group"),
            P("group", None),
        ),
        out_specs=(P("group", "dev"), P("group", "dev", None), P("group", "dev", None)),
        check_vma=False,
    )
```

```python
import functools
import math

import jax
import jax.numpy as jnp
from jax import lax
from jax.experimental import pallas as pl
from jax.experimental.pallas import tpu as pltpu
from jax.sharding import PartitionSpec as P

KVH = 8
HD = 128
QPK = 16
PAGE = 8
GROUPS = 16
DEVS = 32
SPLIT = 4
REQ = 8
RES = 4
CAP = 16
ROWS = RES + CAP
TOKENS = DEVS * PAGE
RES_TOKENS = 512
SHARE = QPK // SPLIT

TINY = 1e-06
LEVEL = 448.0
NONE = -1e30
MESH = pl.DeviceIdType.MESH

CHUNKS = (
    ((0, 0), (0, 1), (1, 0), (1, 1), (7, 0), (7, 1)),
    ((2, 0), (2, 1), (6, 0), (6, 1)),
    ((3, 0), (3, 1), (5, 0), (5, 1)),
    ((4, 0),),
    ((4, 1),),
)
COUNTS = tuple(2 * len(chunk) for chunk in CHUNKS)
LATE = (2, 3, 4)


def attend(queries, keys, values, scales, usable):
    count = len(queries)
    scores = [
        lax.dot_general(
            queries[i], keys[i], (((1,), (1,)), ((), ())), preferred_element_type=jnp.float32
        )
        for i in range(count)
    ]
    scores = [
        jnp.where(usable[i], scores[i] * (scales[i][0] * (1.0 / math.sqrt(HD))), NONE)
        for i in range(count)
    ]
    highest = [jnp.max(each, axis=1, keepdims=True) for each in scores]
    raised = [
        jnp.where(usable[i], jnp.exp(scores[i] - highest[i]), 0.0) for i in range(count)
    ]
    weight_sum = [jnp.sum(each, axis=1, keepdims=True) for each in raised]
    numerator = [
        jnp.dot(
            (raised[i] * scales[i][1]).astype(jnp.bfloat16),
            values[i],
            preferred_element_type=jnp.float32,
        )
        for i in range(count)
    ]
    return numerator, highest, weight_sum


def kernel(
    table_hbm,
    dest_hbm,
    length_hbm,
    res_length_hbm,
    pool_hbm,
    query_hbm,
    res_kv_hbm,
    res_scale_hbm,
    part_got,
    cache_out_ref,
    scale_out_ref,
    table_ref,
    dest_ref,
    length_ref,
    res_length_ref,
    pool_ref,
    query_in,
    res_kv_ref,
    res_scale_ref,
    query_ref,
    send1,
    got1_0,
    got1_1,
    got1_2,
    got1_3,
    got1_4,
    send2_0,
    send2_1,
    send2_2,
    send2_3,
    send2_4,
    got2_0,
    got2_1,
    got2_2,
    got2_3,
    got2_4,
    meta_send,
    meta_got,
    meta_smem,
    picked,
    slot_source,
    slot_length,
    cache,
    scales,
    early_numerator,
    early_highest,
    early_sum,
    scale_rows_ref,
    part_send,
    send1_sem,
    got1_sem,
    send2_sem,
    got2_sem,
    meta_sem,
    part_sem,
    local_sem,
    cache_sem,
    in_sem,
    ready_sem,
):
    got1 = (got1_0, got1_1, got1_2, got1_3, got1_4)
    send2 = (send2_0, send2_1, send2_2, send2_3, send2_4)
    got2 = (got2_0, got2_1, got2_2, got2_3, got2_4)
    group = lax.axis_index("group")
    dev = lax.axis_index("dev")
    x_hi = dev // 16
    pair = (dev % 16) // 2
    parity = dev % 2
    head = dev // SPLIT
    part = dev % SPLIT

    x_parts = (x_hi * 16, (1 - x_hi) * 16)
    pair_parts = [lax.rem(pair + k, 8) * 2 for k in range(8)]
    parities = (parity, 1 - parity)

    def peer_dev(offset, dx, dp):
        return x_parts[dx] + pair_parts[offset] + parities[dp]

    def request_for(target):
        picked = jnp.int32(0)
        for j in range(REQ):
            picked = jnp.where(dest_ref[j] == target, j, picked)
        return picked

    def length_for(target):
        picked = jnp.int32(0)
        for j in range(REQ):
            picked = jnp.where(dest_ref[j] == target, length_ref[j], picked)
        return picked

    loads = [
        pltpu.make_async_copy(source, target, in_sem.at[i])
        for i, (source, target) in enumerate(
            (
                (pool_hbm, pool_ref),
                (table_hbm, table_ref),
                (dest_hbm, dest_ref),
                (length_hbm, length_ref),
                (res_length_hbm, res_length_ref),
                (
                    query_hbm.at[:, pl.ds(pl.multiple_of(head * (QPK * HD), 128), QPK * HD)],
                    query_in,
                ),
                (res_kv_hbm, res_kv_ref),
                (res_scale_hbm, res_scale_ref),
            )
        )
    ]
    for load in loads[:5]:
        load.start()

    barrier = pltpu.get_barrier_semaphore()
    near = [
        (offset, dx, dp)
        for offset, dx in CHUNKS[0]
        for dp in range(2)
        if (offset, dx, dp) != (0, 0, 0)
    ]
    for peer in near:
        pl.semaphore_signal(
            barrier, inc=1, device_id=(group, peer_dev(*peer)), device_id_type=MESH
        )

    @pl.loop(1, GROUPS)
    def _(k):
        pl.semaphore_signal(
            barrier, inc=1, device_id=(lax.rem(group + k, GROUPS), dev), device_id_type=MESH
        )

    for load in loads[:5]:
        load.wait()
    for load in loads[5:]:
        load.start()

    @pl.loop(0, REQ)
    def _(j):
        for s in range(SPLIT):
            page = pool_ref[table_ref[0, 0, j * SPLIT + s]].astype(jnp.float32)
            for h in range(KVH):
                block = jnp.concatenate(
                    [
                        page[:, h * HD : (h + 1) * HD],
                        page[:, (KVH + h) * HD : (KVH + h + 1) * HD],
                    ],
                    axis=0,
                )
                send1[h * SPLIT + s, j] = block.astype(jnp.bfloat16)

    pl.semaphore_wait(barrier, len(near) + GROUPS - 1)

    def start(c):
        for dp in range(2):
            for offset, dx in CHUNKS[c]:
                if (offset, dx, dp) == (0, 0, 0):
                    continue
                to = peer_dev(offset, dx, dp)
                place = CHUNKS[c].index(((8 - offset) % 8, dx)) * 2 + parity
                pltpu.make_async_remote_copy(
                    src_ref=send1.at[to],
                    dst_ref=got1[c].at[place],
                    send_sem=send1_sem,
                    recv_sem=got1_sem.at[c],
                    device_id=(group, to),
                    device_id_type=MESH,
                ).start()

    def round_over(i):
        for offset in (1, 7):
            pl.semaphore_signal(
                ready_sem.at[i],
                inc=1,
                device_id=(group, peer_dev(offset, 0, 0)),
                device_id_type=MESH,
            )

    def await_round(i):
        pl.semaphore_wait(ready_sem.at[i], 2)

    round_over(0)
    start(0)
    await_round(0)
    round_over(1)
    start(1)
    await_round(1)
    round_over(2)
    start(2)
    await_round(2)
    start(3)
    start(4)

    @pl.loop(0, GROUPS)
    def _(g):
        meta_send[g] = jnp.full((1, 128), length_for(g), jnp.int32)
        picked[g] = request_for(g)

    @pl.loop(1, GROUPS)
    def _(k):
        to = lax.rem(group + k, GROUPS)
        pltpu.make_async_remote_copy(
            src_ref=meta_send.at[to],
            dst_ref=meta_got.at[group],
            send_sem=meta_sem.at[0],
            recv_sem=meta_sem.at[1],
            device_id=(to, dev),
            device_id_type=MESH,
        ).start()

    got1[0][parity] = send1[dev]
    meta_got[group] = meta_send[group]

    for load in loads[5:]:
        load.wait()
    heads = query_in[...].astype(jnp.float32)
    for q in range(QPK):
        query_ref[:, q, :] = heads[:, q * HD : (q + 1) * HD]
    lane16 = lax.broadcasted_iota(jnp.int32, (QPK, 128), 1)
    stat_highest = jnp.zeros((QPK, 128), jnp.float32)
    stat_sum = jnp.zeros((QPK, 128), jnp.float32)

    def keep(row, highest, weight_sum, stats):
        here = lane16 == row
        return jnp.where(here, highest, stats[0]), jnp.where(here, weight_sum, stats[1])

    def put(four, numerators):
        for s in range(SPLIT):
            share = [each[s * SHARE : (s + 1) * SHARE] for each in numerators]
            part_send[s, four * 16 : (four + 1) * 16] = jnp.concatenate(share, axis=0).astype(
                part_send.dtype
            )

    stats = (stat_highest, stat_sum)
    res_position = part * RES_TOKENS + lax.broadcasted_iota(jnp.int32, (QPK, RES_TOKENS), 1)
    row_scales = [res_scale_ref[r].astype(jnp.float32) for r in range(RES)]
    numerators, highest, weight_sum = attend(
        [query_ref[r].astype(jnp.bfloat16) for r in range(RES)],
        [res_kv_ref[r, :, :HD] for r in range(RES)],
        [res_kv_ref[r, :, HD:] for r in range(RES)],
        [(each[0:1], each[1:2]) for each in row_scales],
        [res_position < res_length_ref[r] for r in range(RES)],
    )
    for r in range(RES):
        stats = keep(r, highest[r], weight_sum[r], stats)
    put(0, numerators)

    def send_parts(rows):
        for k in range(1, SPLIT):
            s = lax.rem(part + k, SPLIT)
            pltpu.make_async_remote_copy(
                src_ref=part_send.at[s, rows],
                dst_ref=part_got.at[part, rows],
                send_sem=part_sem.at[0],
                recv_sem=part_sem.at[1],
                device_id=(group, head * SPLIT + s),
                device_id_type=MESH,
            ).start()

    send_parts(pl.ds(0, RES * SHARE))

    def rows_of(c):
        return [
            pl.ds(pl.multiple_of((x_parts[dx] + pair_parts[offset]) * PAGE, 16), 16)
            for offset, dx in CHUNKS[c]
        ]

    late_rows = [at for c in LATE for at in rows_of(c)]

    @pl.loop(0, CAP)
    def _(slot):
        for at in late_rows:
            cache[slot, at, :] = jnp.zeros((16, 2 * HD), jnp.bfloat16)
            scales[slot, at, :] = jnp.zeros((16, 128), jnp.bfloat16)

    def forward(c):
        count = COUNTS[c]
        taken = count - 1 if c == 0 else count
        arrived = got1[c].at[pl.ds(0, taken)]
        pltpu.make_async_copy(arrived, arrived, got1_sem.at[c]).wait()
        got2[c][group] = got1[c][:, picked[group]]

        @pl.loop(0, 3)
        def _(third):
            targets = [lax.rem(group + third * 5 + k, GROUPS) for k in range(1, 6)]
            for to in targets:
                send2[c][to] = got1[c][:, picked[to]]
            for to in targets:
                pltpu.make_async_remote_copy(
                    src_ref=send2[c].at[to],
                    dst_ref=got2[c].at[group],
                    send_sem=send2_sem.at[c],
                    recv_sem=got2_sem.at[c],
                    device_id=(to, dev),
                    device_id_type=MESH,
                ).start()

    lane_rows = lax.broadcasted_iota(jnp.int32, (16, 128), 1)

    def store(c):
        count = COUNTS[c]
        others = got2[c].at[pl.ds(0, GROUPS - 1)]
        pltpu.make_async_copy(others, others, got2_sem.at[c]).wait()

        places = rows_of(c)

        at_once = 2 if len(places) > 1 else 8

        @pl.loop(0, CAP // at_once)
        def _(some):
            for k in range(at_once):
                slot = some * at_once + k
                present = slot_length[slot] > 0
                block = got2[c][slot_source[slot]].astype(jnp.float32)
                block = jnp.where(present, block, 0.0)
                peak = jnp.max(jnp.abs(block), axis=2, keepdims=True)
                scale = ((peak + TINY) / LEVEL).astype(jnp.bfloat16).astype(jnp.float32)
                stored = block * (1.0 / scale)
                scale = jnp.broadcast_to(jnp.where(present, scale, 0.0), block.shape)
                for i, at in enumerate(places):
                    n = i * 2
                    for kind in range(2):
                        rows = slice(kind * PAGE, (kind + 1) * PAGE)
                        both = jnp.concatenate([stored[n, rows], stored[n + 1, rows]], axis=0)
                        cache[slot, at, kind * HD : (kind + 1) * HD] = both.astype(jnp.bfloat16)
                    key_scale = jnp.concatenate([scale[n, :PAGE], scale[n + 1, :PAGE]], axis=0)
                    value_scale = jnp.concatenate([scale[n, PAGE:], scale[n + 1, PAGE:]], axis=0)
                    scales[slot, at] = jnp.where(lane_rows == 0, key_scale, value_scale).astype(
                        jnp.bfloat16
                    )

        for at in places:
            pltpu.make_async_copy(
                cache.at[:, at, :], cache_out_ref.at[:, at, :], cache_sem
            ).start()

    forward(0)
    forward(1)

    metas = meta_got.at[pl.ds(0, GROUPS - 1)]
    pltpu.make_async_copy(metas, metas, meta_sem.at[1]).wait()
    pltpu.make_async_copy(meta_got, meta_smem, local_sem.at[0]).start()
    pltpu.make_async_copy(meta_got, meta_smem, local_sem.at[0]).wait()

    @pl.loop(0, CAP)
    def _(slot):
        source = jnp.int32(0)
        length = jnp.int32(0)
        rank = jnp.int32(0)
        for g in range(GROUPS):
            this_length = meta_smem[g, 0, 0]
            here = jnp.logical_and(this_length > 0, rank == slot)
            source = jnp.where(here, g, source)
            length = jnp.where(here, this_length, length)
            rank = rank + jnp.where(this_length > 0, 1, 0)
        slot_source[slot] = source
        slot_length[slot] = length

    row16 = lax.broadcasted_iota(jnp.int32, (QPK, 128), 0)
    pick = jnp.where(lane16 == row16 // PAGE, 1.0, 0.0).astype(jnp.bfloat16)

    def scale_rows(block):
        return lax.dot_general(
            pick, block, (((1,), (1,)), ((), ())), preferred_element_type=jnp.float32
        )

    def attend_early():
        index = lax.broadcasted_iota(jnp.int32, (QPK, TOKENS), 1)
        device = index // PAGE
        position = device * (SPLIT * PAGE) + part * PAGE + index % PAGE
        its_pair = (device % 16) // 2
        early = its_pair >= 0
        for c in LATE:
            for offset, _ in CHUNKS[c]:
                early = jnp.logical_and(early, its_pair * 2 != pair_parts[offset])

        @pl.loop(0, CAP // 4)
        def _(four):
            slots = [four * 4 + k for k in range(4)]
            rows = [scale_rows(scales[slot]) for slot in slots]
            numerator, highest, weight_sum = attend(
                [query_ref[RES + slot].astype(jnp.bfloat16) for slot in slots],
                [cache[slot, :, :HD] for slot in slots],
                [cache[slot, :, HD:] for slot in slots],
                [(each[0:1], each[PAGE : PAGE + 1]) for each in rows],
                [jnp.logical_and(early, position < slot_length[slot]) for slot in slots],
            )
            for k, slot in enumerate(slots):
                early_numerator[slot] = numerator[k]
                early_highest[slot] = jnp.broadcast_to(highest[k], (QPK, 128))
                early_sum[slot] = jnp.broadcast_to(weight_sum[k], (QPK, 128))

    def attend_late(stats):
        wide = 16 * len(late_rows)
        index = lax.broadcasted_iota(jnp.int32, (QPK, wide), 1)
        device = jnp.zeros((QPK, wide), jnp.int32)
        n = 0
        for c in LATE:
            for offset, dx in CHUNKS[c]:
                device = jnp.where(index // 16 == n, x_parts[dx] + pair_parts[offset], device)
                n += 1
        device = device + (index % 16) // PAGE
        position = device * (SPLIT * PAGE) + part * PAGE + index % PAGE
        for eight in range(CAP // 8):
            slots = [eight * 8 + k for k in range(8)]
            rows = [
                scale_rows(jnp.concatenate([scales[slot, at, :] for at in late_rows], axis=0))
                for slot in slots
            ]
            tokens = [
                jnp.concatenate([cache[slot, at, :] for at in late_rows], axis=0)
                for slot in slots
            ]
            numerator, highest, weight_sum = attend(
                [query_ref[RES + slot].astype(jnp.bfloat16) for slot in slots],
                [each[:, :HD] for each in tokens],
                [each[:, HD:] for each in tokens],
                [(each[0:1], each[PAGE : PAGE + 1]) for each in rows],
                [position < slot_length[slot] for slot in slots],
            )
            tops = [jnp.maximum(early_highest[slots[k]], highest[k]) for k in range(8)]
            early_factors = [jnp.exp(early_highest[slots[k]] - tops[k]) for k in range(8)]
            factors = [jnp.exp(highest[k] - tops[k]) for k in range(8)]
            numerators = [
                early_numerator[slots[k]] * early_factors[k] + numerator[k] * factors[k]
                for k in range(8)
            ]
            for k in range(8):
                total = early_sum[slots[k]] * early_factors[k] + weight_sum[k] * factors[k]
                stats = keep(RES + slots[k], tops[k], total, stats)
            put(1 + eight * 2, numerators[:4])
            put(2 + eight * 2, numerators[4:])
        return stats

    store(0)
    forward(2)
    store(1)
    forward(3)
    attend_early()
    forward(4)
    store(2)
    store(3)
    store(4)
    stats = attend_late(stats)
    for s in range(SPLIT):
        shares = [each[s * SHARE : (s + 1) * SHARE] for each in stats]
        part_send[s, ROWS * SHARE :] = jnp.concatenate(shares, axis=0)

    send_parts(pl.ds(RES * SHARE, (CAP + 2) * SHARE))
    own_copies = [
        pltpu.make_async_copy(part_send.at[part], part_got.at[part], local_sem.at[3]),
    ]
    for own_copy in own_copies:
        own_copy.start()

    @pl.loop(0, CAP // 4)
    def _(four):
        slots = [four * 4 + k for k in range(4)]
        rows = [scale_rows(scales[slot]).astype(jnp.bfloat16) for slot in slots]
        for k, slot in enumerate(slots):
            scale_rows_ref[slot, 0:1, :] = rows[k][0:1]
            scale_rows_ref[slot, 1:2, :] = rows[k][PAGE : PAGE + 1]

    scale_copy = pltpu.make_async_copy(scale_rows_ref, scale_out_ref, local_sem.at[2])
    scale_copy.start()

    three_parts = part_got.at[pl.ds(0, SPLIT - 1)]
    pltpu.make_async_copy(three_parts, three_parts, part_sem.at[1]).wait()

    sent = send1.at[pl.ds(0, DEVS - 1)]
    pltpu.make_async_copy(sent, sent, send1_sem).wait()
    for c in range(len(CHUNKS)):
        sent = send2[c].at[pl.ds(0, GROUPS - 1)]
        pltpu.make_async_copy(sent, sent, send2_sem.at[c]).wait()
    sent = meta_send.at[pl.ds(0, GROUPS - 1)]
    pltpu.make_async_copy(sent, sent, meta_sem.at[0]).wait()
    sent = part_send.at[pl.ds(0, SPLIT - 1)]
    pltpu.make_async_copy(sent, sent, part_sem.at[0]).wait()
    pltpu.make_async_copy(cache, cache_out_ref, cache_sem).wait()
    scale_copy.wait()
    for own_copy in own_copies:
        own_copy.wait()


def finish_kernel(
    part_in,
    cache_in,
    scale_in,
    attended_out,
    cache_out,
    scale_out,
    part_got,
    attended_ref,
    cache_held,
    scale_held,
    merged_ref,
    in_sem,
    out_sem,
    part_sem,
):
    pieces = [
        (cache_in.at[at], cache_held.at[at], cache_out.at[at])
        for at in (pl.ds(i * 2, 2) for i in range(CAP // 2))
    ]
    pieces.append((scale_in, scale_held, scale_out))
    loads = [pltpu.make_async_copy(p[0], p[1], in_sem.at[i]) for i, p in enumerate(pieces)]
    stores = [pltpu.make_async_copy(p[1], p[2], out_sem.at[i]) for i, p in enumerate(pieces)]
    part_load = pltpu.make_async_copy(part_in, part_got, part_sem.at[0])
    part_load.start()
    for load in loads:
        load.start()
    for load, store in zip(loads, stores):
        load.wait()
        store.start()
    part_load.wait()
    highest = [part_got[s, ROWS * SHARE : (ROWS + 1) * SHARE] for s in range(SPLIT)]
    top = functools.reduce(jnp.maximum, highest)
    factors = [jnp.exp(each - top) for each in highest]
    total = functools.reduce(jnp.add, [part_got[s, (ROWS + 1) * SHARE :] * factors[s] for s in range(SPLIT)])
    total = jnp.maximum(total, 1.0)
    factors = [each / total for each in factors]
    parts = [part_got[s] for s in range(SPLIT)]
    for r in range(ROWS):
        merged = functools.reduce(
            jnp.add,
            [
                parts[s][r * SHARE : (r + 1) * SHARE] * factors[s][:, r : r + 1]
                for s in range(SPLIT)
            ],
        )
        for q in range(SHARE):
            merged_ref[r : r + 1, q * HD : (q + 1) * HD] = merged[q : q + 1]
    attended_ref[...] = merged_ref[...].astype(jnp.bfloat16)
    attended_store = pltpu.make_async_copy(attended_ref, attended_out, part_sem.at[1])
    attended_store.start()
    for store in stores:
        store.wait()
    attended_store.wait()


def body(
    prefill_pool,
    page_table,
    req_lengths,
    dest_group,
    resident_kv,
    resident_scale,
    res_lengths,
    queries,
):
    hbm = pl.BlockSpec(memory_space=pltpu.HBM)
    bf16 = jnp.bfloat16
    cache_shape = jax.ShapeDtypeStruct((CAP, TOKENS, 2 * HD), bf16)
    scale_shape = jax.ShapeDtypeStruct((CAP, 2, TOKENS), bf16)
    part_shape = jax.ShapeDtypeStruct((SPLIT, (ROWS + 2) * SHARE, HD), jnp.float32)
    attended_shape = jax.ShapeDtypeStruct((ROWS, SHARE * HD), bf16)
    results = pl.pallas_call(
        kernel,
        out_shape=(part_shape, cache_shape, scale_shape),
        in_specs=[hbm] * 8,
        out_specs=(hbm,) * 3,
        scratch_shapes=[
            pltpu.SMEM((1, 1, REQ * SPLIT), jnp.int32),
            pltpu.SMEM((REQ,), jnp.int32),
            pltpu.SMEM((REQ,), jnp.int32),
            pltpu.SMEM((RES,), jnp.int32),
            pltpu.VMEM((REQ * SPLIT, PAGE, 2 * KVH * HD), bf16),
            pltpu.VMEM((ROWS, QPK * HD), bf16),
            pltpu.VMEM((RES, RES_TOKENS, 2 * HD), bf16),
            pltpu.VMEM((RES, 2, RES_TOKENS), bf16),
            pltpu.VMEM((ROWS, QPK, HD), jnp.float32),
            pltpu.VMEM((DEVS, REQ, 2 * PAGE, HD), bf16),
            *[pltpu.VMEM((n, REQ, 2 * PAGE, HD), bf16) for n in COUNTS],
            *[pltpu.VMEM((GROUPS, n, 2 * PAGE, HD), bf16) for n in COUNTS],
            *[pltpu.VMEM((GROUPS, n, 2 * PAGE, HD), bf16) for n in COUNTS],
            pltpu.VMEM((GROUPS, 1, 128), jnp.int32),
            pltpu.VMEM((GROUPS, 1, 128), jnp.int32),
            pltpu.SMEM((GROUPS, 1, 128), jnp.int32),
            pltpu.SMEM((GROUPS,), jnp.int32),
            pltpu.SMEM((CAP,), jnp.int32),
            pltpu.SMEM((CAP,), jnp.int32),
            pltpu.VMEM((CAP, TOKENS, 2 * HD), bf16),
            pltpu.VMEM((CAP, TOKENS, 128), bf16),
            *[pltpu.VMEM((CAP, QPK, HD), jnp.float32)] * 3,
            pltpu.VMEM((CAP, 2, TOKENS), bf16),
            pltpu.VMEM(part_shape.shape, part_shape.dtype),
            pltpu.SemaphoreType.DMA,
            pltpu.SemaphoreType.DMA((len(CHUNKS),)),
            pltpu.SemaphoreType.DMA((len(CHUNKS),)),
            pltpu.SemaphoreType.DMA((len(CHUNKS),)),
            pltpu.SemaphoreType.DMA((2,)),
            pltpu.SemaphoreType.DMA((2,)),
            pltpu.SemaphoreType.DMA((4,)),
            pltpu.SemaphoreType.DMA,
            pltpu.SemaphoreType.DMA((8,)),
            pltpu.SemaphoreType.REGULAR((3,)),
        ],
        compiler_params=pltpu.CompilerParams(
            collective_id=0, has_side_effects=True, vmem_limit_bytes=62 * 2**20
        ),
        name="migrate_and_attend",
    )(
        page_table,
        dest_group,
        req_lengths,
        res_lengths,
        prefill_pool,
        queries,
        resident_kv,
        jnp.swapaxes(resident_scale, 1, 2),
    )
    held = (part_shape, attended_shape, cache_shape, scale_shape)
    attended, migrated_cache, migrated_scale = pl.pallas_call(
        finish_kernel,
        out_shape=(attended_shape, cache_shape, scale_shape),
        in_specs=[hbm] * 3,
        out_specs=(hbm,) * 3,
        scratch_shapes=[
            *[pltpu.VMEM(each.shape, each.dtype) for each in held],
            pltpu.VMEM(attended_shape.shape, jnp.float32),
            pltpu.SemaphoreType.DMA((CAP // 2 + 1,)),
            pltpu.SemaphoreType.DMA((CAP // 2 + 1,)),
            pltpu.SemaphoreType.DMA((2,)),
        ],
        compiler_params=pltpu.CompilerParams(vmem_limit_bytes=62 * 2**20),
        name="merge_and_copy",
    )(*results)
    return attended, migrated_cache, jnp.swapaxes(migrated_scale, 1, 2)


def solution(mesh):
    return jax.shard_map(
        body,
        mesh=mesh,
        in_specs=(
            P("group", "dev", None),
            P("group", "dev", None),
            P("group"),
            P("group"),
            P("group", "dev", None),
            P("group", "dev", None),
            P("group"),
            P("group", None),
        ),
        out_specs=(P("group", "dev"), P("group", "dev", None), P("group", "dev", None)),
        check_vma=False,
    )
```
